512 devices in a mesh: row: 32 (over z, core), col: 16 (over x, y).
Axes of the slice: x: 4, y: 4, z: 16, core: 2. Of those that a mesh axis runs over, the one named last changes fastest.
Arguments:
- rhs: bfloat16 [3, 32, 64, 256], P(None, 'row'), may hold values from -6 to 6
- dinv: bfloat16 [3, 32, 256, 256], P(None, 'row'), as said below
- tiles: bfloat16 [2, 32, 32, 256, 256], P(None, 'row', 'col'), may hold values from -0.046875 to 0.046875
- pattern: int32 [2, 2, 32, 32], P(None, None, 'row', 'col'), may hold values from 0 to 31, as said below
Outputs:
- solution: float32 [3, 32, 64, 256], P(None, 'row')
The draws below stay inside these ranges and needn't reach their ends.
Inputs may be any that keep to these rules, and one draw needn't show every extreme that they name: pattern[0, l, p, t] = p; pattern[1, l, p, t] = j has (j) modulo the size of col equal to t // 2; positions may repeat, and repeated tiles add. `dinv`: lower triangular with a positive diagonal.
All inputs are finite; a program needn't handle non-finite values.
Results may differ from the reference program's by a relative error of at most 0.0055.
Values may be sent and summed in bfloat16 or wider, within the bound.
A program may use at most 64 MiB of HBM per device.

```python
import math
import jax
import jax.numpy as jnp
from jax import lax

BS = 256
NRHS = 64
LEVELS = 3
ROWS_DEV = 1
SLOTS = 2
N_ROW = 32
N_COL = 16


def draw_dinv(key, part):
    key_diag, key_off = jax.random.split(jax.random.fold_in(key, 3))
    block_rows = ROWS_DEV * N_ROW
    array_shape = (LEVELS, block_rows, BS, BS)
    diagonal = jnp.exp(jax.random.uniform(key_diag, (LEVELS, block_rows, BS), jnp.float32, math.log(0.5), math.log(2.0)))
    lower = jax.random.normal(key_off, array_shape, jnp.float32) * (0.5 / math.sqrt(BS))
    row_ids = jnp.arange(BS, dtype=jnp.int32)[:, None]
    col_ids = jnp.arange(BS, dtype=jnp.int32)[None, :]
    strict = (col_ids < row_ids).astype(jnp.float32)
    identity = (col_ids == row_ids).astype(jnp.float32)
    matrix = lower * strict + identity * diagonal[..., None]
    return matrix.astype(jnp.bfloat16)


def draw_pattern(key, part):
    key_row, key_group, key_col = jax.random.split(jax.random.fold_in(key, 11), 3)
    array_shape = (LEVELS - 1, N_ROW, N_COL * SLOTS)
    block_rows = ROWS_DEV * N_ROW
    device_row = jnp.arange(N_ROW, dtype=jnp.int32)[None, :, None]
    device_col = (jnp.arange(N_COL * SLOTS, dtype=jnp.int32) // SLOTS)[None, None, :]
    row_offset = jax.random.randint(key_row, array_shape, 0, ROWS_DEV)
    group_pick = jax.random.randint(key_group, array_shape, 0, N_ROW // N_COL)
    col_offset = jax.random.randint(key_col, array_shape, 0, ROWS_DEV)
    row_values = device_row * ROWS_DEV + row_offset
    col_values = (device_col + N_COL * group_pick) * ROWS_DEV + col_offset
    row_values = row_values.at[0, 0, 0].set(0).at[0, N_ROW - 1, 0].set(block_rows - 1)
    col_values = col_values.at[0, 0, 0].set(0).at[0, 0, N_COL * SLOTS - 1].set(block_rows - 1)
    return jnp.stack([row_values, col_values]).astype(jnp.int32)


def block_levels(key, dims, pieces, low, largest):
    def one(position, shards_of):
        draws = jax.random.uniform(jax.random.fold_in(jax.random.fold_in(key, 6), position), (shards_of,), jnp.float32, low / len(pieces), largest / len(pieces))
        return jnp.repeat(jnp.exp(draws), dims[position] // shards_of).reshape((-1,) + (1,) * (len(dims) - position - 1))

    level = one(*pieces[0])
    for cut in pieces[1:]:
        level = level * one(*cut)
    return level


def gaussian(rng, shape, scale, reach, shards=(), kind=jnp.bfloat16):
    array = scale * jax.random.normal(rng, shape, jnp.float32)
    if shards:
        array = array * block_levels(rng, shape, shards, -0.22, 0.18)
    return jnp.clip(array, -reach, reach).astype(kind)


def setup_inputs(seed: int = 0) -> dict:
    seeds = jax.random.split(jax.random.key(seed), 5)
    rhs = gaussian(seeds[0], (LEVELS, ROWS_DEV * N_ROW, NRHS, BS), 1.0, 6.0, ((1, 32),))
    dinv = draw_dinv(jax.random.fold_in(seeds[4], 71), 0)
    tiles = gaussian(seeds[2], (LEVELS - 1, N_ROW, N_COL * SLOTS, BS, BS), (2 * BS * SLOTS * N_COL // ROWS_DEV) ** -0.5, 0.046875, ((1, 32), (2, 16)))
    pattern = draw_pattern(jax.random.fold_in(seeds[4], 71), 0)
    return {"rhs": rhs, "dinv": dinv, "tiles": tiles, "pattern": pattern}


def reference(rhs, dinv, tiles, pattern):
    block_rows = ROWS_DEV * N_ROW
    row_index = pattern[0].reshape(LEVELS - 1, -1)
    col_index = pattern[1].reshape(LEVELS - 1, -1)
    factor_tiles = tiles.reshape(LEVELS - 1, -1, BS, BS)
    forward_list = []
    previous = None
    for level_now in range(LEVELS):
        current = rhs[level_now].astype(jnp.float32)
        if level_now > 0:
            source = previous[col_index[level_now - 1]].astype(jnp.float32)
            product = jnp.einsum("mjb,mab->mja", source, factor_tiles[level_now - 1].astype(jnp.float32), precision=lax.Precision.HIGHEST)
            updates = jnp.zeros((block_rows, NRHS, BS), jnp.float32).at[row_index[level_now - 1]].add(product)
            current = current - updates
        rounded = lax.optimization_barrier(current.astype(jnp.bfloat16)).astype(jnp.float32)
        solved = jnp.einsum("wjb,wab->wja", rounded, dinv[level_now].astype(jnp.float32), precision=lax.Precision.HIGHEST)
        forward_list.append(solved)
        previous = solved.astype(jnp.bfloat16)
    backward_list = [None] * LEVELS
    following = None
    for level_now in range(LEVELS - 1, -1, -1):
        remainder = forward_list[level_now]
        if level_now < LEVELS - 1:
            source = following[row_index[level_now]].astype(jnp.float32)
            product = jnp.einsum("mja,mab->mjb", source, factor_tiles[level_now].astype(jnp.float32), precision=lax.Precision.HIGHEST)
            updates = jnp.zeros((block_rows, NRHS, BS), jnp.float32).at[col_index[level_now]].add(product)
            remainder = remainder - updates
        rounded = lax.optimization_barrier(remainder.astype(jnp.bfloat16)).astype(jnp.float32)
        solved = jnp.einsum("wjb,wba->wja", rounded, dinv[level_now].astype(jnp.float32), precision=lax.Precision.HIGHEST)
        backward_list[level_now] = solved
        following = solved.astype(jnp.bfloat16)
    return jnp.stack(backward_list)
```

```python
import functools

import jax
import jax.numpy as jnp
from jax import lax
from jax.experimental import pallas as pl
from jax.experimental.pallas import tpu as pltpu
from jax.sharding import PartitionSpec as P

MESH = pl.DeviceIdType.MESH
BF16, F32 = jnp.bfloat16, jnp.float32
NT = (((1,), (1,)), ((), ()))
NN = (((1,), (0,)), ((), ()))


def mm(a, b, dims):
    return lax.dot_general(a, b, dims, preferred_element_type=F32)


def kernel(
    dims,
    pat, rhs_hbm, dinv_hbm, tiles_hbm, out,
    rhs, dinv, tiles, load_sem,
    fwd, own, spread, part, red_f, gath, back, red_b,
    self_sem, send_sem, recv_sem,
):
    levels, rows, cols, rep, groups, gr, bs = dims
    nrhs = groups * gr
    slots = tiles.shape[1]
    me_r, me_c = lax.axis_index("row"), lax.axis_index("col")
    side, g_own = lax.rem(me_r, 2), me_c // 2
    home = lax.rem(me_r, cols)
    blk_own = me_r // cols
    is_owner = lax.rem(me_c, 2) == side
    at_home = home == me_c

    loads = [
        pltpu.make_async_copy(rhs_hbm.at[:, g_own], rhs, load_sem.at[0]),
        pltpu.make_async_copy(dinv_hbm, dinv, load_sem.at[1]),
        pltpu.make_async_copy(tiles_hbm, tiles, load_sem.at[2]),
    ]
    for load in loads:
        load.start()

    barrier = pltpu.get_barrier_semaphore()

    def tell(r, c):
        pl.semaphore_signal(barrier, inc=1, device_id=(r, c), device_id_type=MESH)

    def loop(n, body):
        for k in range(n):
            body(k)

    for blk in range(rep):
        def from_owner(k, blk=blk):
            tell(me_c + cols * blk, 2 * lax.rem(g_own + k, groups) + lax.rem(me_c, 2))

        loop(groups, from_owner)
    loop(groups, lambda k: tell(me_r, 2 * lax.rem(g_own + k, groups) + side))

    @pl.when(is_owner)
    def _():
        loop(cols, lambda k: tell(me_r, lax.rem(me_c + k, cols)))
        loop(rows, lambda k: tell(lax.rem(me_r + k, rows), home))
        pl.semaphore_wait(barrier, rows + cols + groups + rep * groups)

    @pl.when(jnp.logical_not(is_owner))
    def _():
        pl.semaphore_wait(barrier, groups + rep * groups)

    def send(src, dst, phase, r, c):
        pltpu.make_async_remote_copy(
            src_ref=src, dst_ref=dst, send_sem=send_sem.at[phase], recv_sem=recv_sem.at[phase],
            device_id=(r, c), device_id_type=MESH,
        ).start()

    def keep(src, dst, phase):
        pltpu.make_async_copy(src, dst, recv_sem.at[phase]).start()

    def arrived(ref, phase):
        pltpu.make_async_copy(ref, ref, recv_sem.at[phase]).wait()

    def sent(ref, phase):
        pltpu.make_async_copy(ref, ref, send_sem.at[phase]).wait()


    phase = 0
    loads[0].wait()
    loads[1].wait()

    for level in range(levels):
        if level == 0:
            @pl.when(is_owner)
            def _():
                fwd[0] = mm(rhs[0], dinv[0], NT)
        else:
            sp, ph_s, ph_r = level - 1, phase, phase + 1
            phase += 2

            @pl.when(is_owner)
            def _(sp=sp, ph_s=ph_s):
                own[sp] = fwd[sp].astype(BF16)
                src, dst = own.at[sp], spread[sp].at[blk_own, g_own]

                def one(k):
                    send(src, dst, ph_s, lax.rem(me_r + k, rows), home)

                for k in range(1, rows):
                    one((k + rows // 2 - 1) % (rows - 1) + 1)

                @pl.when(at_home)
                def _():
                    keep(src, dst, ph_s)

                @pl.when(jnp.logical_not(at_home))
                def _():
                    one(0)

            if level == 1:
                loads[2].wait()
            arrived(spread[sp], ph_s)
            total = None
            for slot in range(slots):
                blk = pat[1, sp, slot] // cols
                source = spread[sp][blk].astype(F32).reshape(nrhs, bs).astype(BF16)
                product = mm(source, tiles[sp, slot], NT)
                total = product if total is None else total + product
            part[sp, 0] = total.astype(BF16).reshape(groups, gr, bs)

            def one(k, sp=sp, ph_r=ph_r):
                g = lax.rem(g_own + k, groups)
                send(part.at[sp, 0, g], red_f.at[sp, me_c], ph_r, me_r, 2 * g + side)

            for k in range(1, groups):
                one(k)

            @pl.when(jnp.logical_not(is_owner))
            def _(one=one):
                one(0)

            @pl.when(is_owner)
            def _(sp=sp, ph_r=ph_r, level=level):
                keep(part.at[sp, 0, g_own], red_f.at[sp, me_c], ph_r)
                arrived(red_f.at[sp], ph_r)
                update = jnp.sum(red_f[sp].astype(F32), axis=0)
                current = rhs[level].astype(F32) - update
                fwd[level] = mm(current.astype(BF16), dinv[level], NT)

    for level in range(levels - 1, -1, -1):
        ph_r = phase
        phase += 1

        @pl.when(is_owner)
        def _(level=level, ph_r=ph_r):
            remainder = fwd[level]
            if level < levels - 1:
                arrived(red_b.at[level], ph_r - 1)
                remainder = remainder - jnp.sum(red_b[level].astype(F32), axis=0)
            back[level] = mm(remainder.astype(BF16), dinv[level], NN)
            src, dst = back.at[level], gath.at[level, g_own]
            for k in range(1, cols):
                send(src, dst, ph_r, me_r, lax.rem(me_c + k, cols))
            keep(src, dst, ph_r)

        arrived(gath.at[level], ph_r)
        if level > 0:
            lo, ph_b = level - 1, phase
            phase += 1
            source = gath[level].reshape(nrhs, bs).astype(BF16)
            products = [mm(source, tiles[lo, slot], NN) for slot in range(slots)]
            for blk in range(rep):
                total = None
                for slot in range(slots):
                    hit = pat[1, lo, slot] // cols == blk
                    term = jnp.where(hit, products[slot], 0.0)
                    total = term if total is None else total + term
                part[levels - 1 + lo, blk] = total.astype(BF16).reshape(groups, gr, bs)
            for k in range(groups):
                for blk in range(rep):
                    g = lax.rem(g_own + k, groups)
                    row = me_c + cols * blk
                    src, dst = part.at[levels - 1 + lo, blk, g], red_b.at[lo, me_r]
                    if k:
                        send(src, dst, ph_b, row, 2 * g + lax.rem(me_c, 2))
                    else:
                        @pl.when(row == me_r)
                        def _(src=src, dst=dst, ph_b=ph_b):
                            keep(src, dst, ph_b)

                        @pl.when(row != me_r)
                        def _(src=src, dst=dst, ph_b=ph_b, row=row):
                            send(src, dst, ph_b, row, me_c)
        out[level] = gath[level]

    phase = 0
    for level in range(1, levels):
        @pl.when(is_owner)
        def _(phase=phase):
            n = rows - 1
            sent(red_b.at[0, pl.ds(0, n)], phase)
            sent(red_f.at[0, pl.ds(0, groups - 1)], phase + 1)

            @pl.when(jnp.logical_not(at_home))
            def _():
                sent(red_b.at[0, 0], phase)

        @pl.when(jnp.logical_not(is_owner))
        def _(phase=phase):
            sent(red_f.at[0, pl.ds(0, groups)], phase + 1)

        phase += 2
    for level in range(levels - 1, -1, -1):
        @pl.when(is_owner)
        def _(phase=phase):
            for k in range(cols - 1):
                sent(gath.at[0, 0], phase)

        phase += 1
        if level > 0:
            sent(red_b.at[0, pl.ds(0, rep * groups - 1)], phase)

            @pl.when(jnp.logical_not(at_home))
            def _(phase=phase):
                sent(red_b.at[0, 0], phase)

            phase += 1


def per_device(rhs, dinv, tiles, pattern):
    levels, _, nrhs, bs = rhs.shape
    rows, cols = lax.axis_size("row"), lax.axis_size("col")
    rep, groups = rows // cols, cols // 2
    gr, slots = nrhs // groups, tiles.shape[2]
    pairs = levels - 1
    phases = 2 * pairs + levels + pairs
    out = pl.pallas_call(
        functools.partial(kernel, (levels, rows, cols, rep, groups, gr, bs)),
        out_shape=jax.ShapeDtypeStruct((levels, groups, gr, bs), F32),
        in_specs=[pl.BlockSpec(memory_space=pltpu.SMEM)] + [pl.BlockSpec(memory_space=pl.ANY)] * 3,
        out_specs=pl.BlockSpec(memory_space=pltpu.VMEM),
        scratch_shapes=[
            pltpu.VMEM((levels, gr, bs), BF16),
            pltpu.VMEM((levels, bs, bs), BF16),
            pltpu.VMEM((pairs, slots, bs, bs), BF16),
            pltpu.SemaphoreType.DMA((3,)),
            pltpu.VMEM((levels, gr, bs), F32),
            pltpu.VMEM((pairs, gr, bs), BF16),
            [pltpu.VMEM((rep, groups, gr, bs), BF16) for _ in range(pairs)],
            pltpu.VMEM((2 * pairs, rep, groups, gr, bs), BF16),
            pltpu.VMEM((pairs, cols, gr, bs), BF16),
            pltpu.VMEM((levels, groups, gr, bs), F32),
            pltpu.VMEM((levels, gr, bs), F32),
            pltpu.VMEM((pairs, rows, gr, bs), BF16),
            pltpu.SemaphoreType.DMA((1,)),
            pltpu.SemaphoreType.DMA((phases,)),
            pltpu.SemaphoreType.DMA((phases,)),
        ],
        compiler_params=pltpu.CompilerParams(
            collective_id=0, has_side_effects=True, vmem_limit_bytes=16 * 2**20
        ),
    )(
        pattern[:, :, 0, :],
        rhs.reshape(levels, groups, gr, bs),
        dinv.reshape(levels, bs, bs),
        tiles.reshape(pairs, slots, bs, bs),
    )
    return out.reshape(levels, 1, nrhs, bs)


def solution(mesh):
    in_specs = (
        P(None, "row", None, None),
        P(None, "row", None, None),
        P(None, "row", "col", None, None),
        P(None, None, "row", "col"),
    )
    return jax.shard_map(
        per_device, mesh=mesh, in_specs=in_specs, out_specs=P(None, "row", None, None), check_vma=False
    )
```

```python
import functools

import jax
import jax.numpy as jnp
from jax import lax
from jax.experimental import pallas as pl
from jax.experimental.pallas import tpu as pltpu
from jax.sharding import PartitionSpec as P

MESH = pl.DeviceIdType.MESH
BF16, F32 = jnp.bfloat16, jnp.float32
NT = (((1,), (1,)), ((), ()))
NN = (((1,), (0,)), ((), ()))


def mm(a, b, dims):
    return lax.dot_general(a, b, dims, preferred_element_type=F32)


def kernel(
    dims,
    pat, rhs_hbm, dinv_hbm, tiles_hbm, out,
    rhs, dinv, tiles, load_sem,
    fwd, own, spread, part, red_f, gath, back, red_b,
    self_sem, send_sem, recv_sem,
):
    levels, rows, cols, rep, groups, gr, bs = dims
    nrhs = groups * gr
    slots = tiles.shape[1]
    me_r, me_c = lax.axis_index("row"), lax.axis_index("col")
    side, g_own = lax.rem(me_r, 2), me_c // 2
    home = lax.rem(me_r, cols)
    blk_own = me_r // cols
    is_owner = lax.rem(me_c, 2) == side
    at_home = home == me_c

    loads = [
        pltpu.make_async_copy(rhs_hbm.at[:, g_own], rhs, load_sem.at[0]),
        pltpu.make_async_copy(dinv_hbm, dinv, load_sem.at[1]),
        pltpu.make_async_copy(tiles_hbm, tiles, load_sem.at[2]),
    ]
    for load in loads:
        load.start()

    barrier = pltpu.get_barrier_semaphore()

    def tell(r, c):
        pl.semaphore_signal(barrier, inc=1, device_id=(r, c), device_id_type=MESH)

    def loop(n, body):
        for k in range(n):
            body(k)

    with jax.named_scope("tell"):
        for blk in range(rep):
            def from_owner(k, blk=blk):
                tell(me_c + cols * blk, 2 * lax.rem(g_own + k, groups) + lax.rem(me_c, 2))

            loop(groups, from_owner)
        loop(groups, lambda k: tell(me_r, 2 * lax.rem(g_own + k, groups) + side))

    with jax.named_scope("meet"):
        @pl.when(is_owner)
        def _():
            loop(cols, lambda k: tell(me_r, lax.rem(me_c + k, cols)))
            loop(rows, lambda k: tell(lax.rem(me_r + k, rows), home))
            pl.semaphore_wait(barrier, rows + cols + groups + rep * groups)

        @pl.when(jnp.logical_not(is_owner))
        def _():
            pl.semaphore_wait(barrier, groups + rep * groups)

    def send(src, dst, phase, r, c):
        pltpu.make_async_remote_copy(
            src_ref=src, dst_ref=dst, send_sem=send_sem.at[phase], recv_sem=recv_sem.at[phase],
            device_id=(r, c), device_id_type=MESH,
        ).start()

    def keep(src, dst, phase):
        pltpu.make_async_copy(src, dst, recv_sem.at[phase]).start()

    def arrived(ref, phase):
        pltpu.make_async_copy(ref, ref, recv_sem.at[phase]).wait()

    def sent(ref, phase):
        pltpu.make_async_copy(ref, ref, send_sem.at[phase]).wait()


    phase = 0
    loads[0].wait()
    loads[1].wait()

    for level in range(levels):
        if level == 0:
            @pl.when(is_owner)
            def _():
                fwd[0] = mm(rhs[0], dinv[0], NT)
        else:
            sp, ph_s, ph_r = level - 1, phase, phase + 1
            phase += 2

            with jax.named_scope("spread"):
                @pl.when(is_owner)
                def _(sp=sp, ph_s=ph_s):
                    own[sp] = fwd[sp].astype(BF16)
                    src, dst = own.at[sp], spread[sp].at[blk_own, g_own]

                    def one(k):
                        send(src, dst, ph_s, lax.rem(me_r + k, rows), home)

                    for k in range(1, rows):
                        one((k + rows // 2 - 1) % (rows - 1) + 1)

                    @pl.when(at_home)
                    def _():
                        keep(src, dst, ph_s)

                    @pl.when(jnp.logical_not(at_home))
                    def _():
                        one(0)

            if level == 1:
                loads[2].wait()
            with jax.named_scope("spread_wait"):
                arrived(spread[sp], ph_s)
            with jax.named_scope("tiles"):
                total = None
                for slot in range(slots):
                    blk = pat[1, sp, slot] // cols
                    source = spread[sp][blk].astype(F32).reshape(nrhs, bs).astype(BF16)
                    product = mm(source, tiles[sp, slot], NT)
                    total = product if total is None else total + product
                part[sp, 0] = total.astype(BF16).reshape(groups, gr, bs)

            def one(k, sp=sp, ph_r=ph_r):
                g = lax.rem(g_own + k, groups)
                send(part.at[sp, 0, g], red_f.at[sp, me_c], ph_r, me_r, 2 * g + side)

            with jax.named_scope("reduce"):
                for k in range(1, groups):
                    one(k)

            @pl.when(jnp.logical_not(is_owner))
            def _(one=one):
                one(0)

            @pl.when(is_owner)
            def _(sp=sp, ph_r=ph_r, level=level):
                keep(part.at[sp, 0, g_own], red_f.at[sp, me_c], ph_r)
                with jax.named_scope("reduce_wait"):
                    arrived(red_f.at[sp], ph_r)
                update = jnp.sum(red_f[sp].astype(F32), axis=0)
                current = rhs[level].astype(F32) - update
                fwd[level] = mm(current.astype(BF16), dinv[level], NT)

    for level in range(levels - 1, -1, -1):
        ph_r = phase
        phase += 1

        @pl.when(is_owner)
        def _(level=level, ph_r=ph_r):
            remainder = fwd[level]
            if level < levels - 1:
                with jax.named_scope("reduce_wait"):
                    arrived(red_b.at[level], ph_r - 1)
                remainder = remainder - jnp.sum(red_b[level].astype(F32), axis=0)
            back[level] = mm(remainder.astype(BF16), dinv[level], NN)
            src, dst = back.at[level], gath.at[level, g_own]
            with jax.named_scope("gather"):
                for k in range(1, cols):
                    send(src, dst, ph_r, me_r, lax.rem(me_c + k, cols))
            keep(src, dst, ph_r)

        with jax.named_scope("gather_wait"):
            arrived(gath.at[level], ph_r)
        if level > 0:
            lo, ph_b = level - 1, phase
            phase += 1
            with jax.named_scope("tiles"):
                source = gath[level].reshape(nrhs, bs).astype(BF16)
                products = [mm(source, tiles[lo, slot], NN) for slot in range(slots)]
                for blk in range(rep):
                    total = None
                    for slot in range(slots):
                        hit = pat[1, lo, slot] // cols == blk
                        term = jnp.where(hit, products[slot], 0.0)
                        total = term if total is None else total + term
                    part[levels - 1 + lo, blk] = total.astype(BF16).reshape(groups, gr, bs)
            with jax.named_scope("reduce"):
                for k in range(groups):
                    for blk in range(rep):
                        g = lax.rem(g_own + k, groups)
                        row = me_c + cols * blk
                        src, dst = part.at[levels - 1 + lo, blk, g], red_b.at[lo, me_r]
                        if k:
                            send(src, dst, ph_b, row, 2 * g + lax.rem(me_c, 2))
                        else:
                            @pl.when(row == me_r)
                            def _(src=src, dst=dst, ph_b=ph_b):
                                keep(src, dst, ph_b)

                            @pl.when(row != me_r)
                            def _(src=src, dst=dst, ph_b=ph_b, row=row):
                                send(src, dst, ph_b, row, me_c)
        out[level] = gath[level]

    with jax.named_scope("drain"):
        phase = 0
        for level in range(1, levels):
            @pl.when(is_owner)
            def _(phase=phase):
                n = rows - 1
                sent(red_b.at[0, pl.ds(0, n)], phase)
                sent(red_f.at[0, pl.ds(0, groups - 1)], phase + 1)

                @pl.when(jnp.logical_not(at_home))
                def _():
                    sent(red_b.at[0, 0], phase)

            @pl.when(jnp.logical_not(is_owner))
            def _(phase=phase):
                sent(red_f.at[0, pl.ds(0, groups)], phase + 1)

            phase += 2
        for level in range(levels - 1, -1, -1):
            @pl.when(is_owner)
            def _(phase=phase):
                for k in range(cols - 1):
                    sent(gath.at[0, 0], phase)

            phase += 1
            if level > 0:
                sent(red_b.at[0, pl.ds(0, rep * groups - 1)], phase)

                @pl.when(jnp.logical_not(at_home))
                def _(phase=phase):
                    sent(red_b.at[0, 0], phase)

                phase += 1


def per_device(rhs, dinv, tiles, pattern):
    levels, _, nrhs, bs = rhs.shape
    rows, cols = lax.axis_size("row"), lax.axis_size("col")
    rep, groups = rows // cols, cols // 2
    gr, slots = nrhs // groups, tiles.shape[2]
    pairs = levels - 1
    phases = 2 * pairs + levels + pairs
    out = pl.pallas_call(
        functools.partial(kernel, (levels, rows, cols, rep, groups, gr, bs)),
        out_shape=jax.ShapeDtypeStruct((levels, groups, gr, bs), F32),
        in_specs=[pl.BlockSpec(memory_space=pltpu.SMEM)] + [pl.BlockSpec(memory_space=pl.ANY)] * 3,
        out_specs=pl.BlockSpec(memory_space=pltpu.VMEM),
        scratch_shapes=[
            pltpu.VMEM((levels, gr, bs), BF16),
            pltpu.VMEM((levels, bs, bs), BF16),
            pltpu.VMEM((pairs, slots, bs, bs), BF16),
            pltpu.SemaphoreType.DMA((3,)),
            pltpu.VMEM((levels, gr, bs), F32),
            pltpu.VMEM((pairs, gr, bs), BF16),
            [pltpu.VMEM((rep, groups, gr, bs), BF16) for _ in range(pairs)],
            pltpu.VMEM((2 * pairs, rep, groups, gr, bs), BF16),
            pltpu.VMEM((pairs, cols, gr, bs), BF16),
            pltpu.VMEM((levels, groups, gr, bs), F32),
            pltpu.VMEM((levels, gr, bs), F32),
            pltpu.VMEM((pairs, rows, gr, bs), BF16),
            pltpu.SemaphoreType.DMA((1,)),
            pltpu.SemaphoreType.DMA((phases,)),
            pltpu.SemaphoreType.DMA((phases,)),
        ],
        compiler_params=pltpu.CompilerParams(
            collective_id=0, has_side_effects=True
        ),
    )(
        pattern[:, :, 0, :],
        rhs.reshape(levels, groups, gr, bs),
        dinv.reshape(levels, bs, bs),
        tiles.reshape(pairs, slots, bs, bs),
    )
    return out.reshape(levels, 1, nrhs, bs)


def solution(mesh):
    in_specs = (
        P(None, "row", None, None),
        P(None, "row", None, None),
        P(None, "row", "col", None, None),
        P(None, None, "row", "col"),
    )
    return jax.shard_map(
        per_device, mesh=mesh, in_specs=in_specs, out_specs=P(None, "row", None, None), check_vma=False
    )
```

```python
import functools

import jax
import jax.numpy as jnp
from jax import lax
from jax.experimental import pallas as pl
from jax.experimental.pallas import tpu as pltpu
from jax.sharding import PartitionSpec as P

MESH = pl.DeviceIdType.MESH
BF16, F32 = jnp.bfloat16, jnp.float32
NT = (((1,), (1,)), ((), ()))
NN = (((1,), (0,)), ((), ()))
NY = 4


def mm(a, b, dims):
    return lax.dot_general(a, b, dims, preferred_element_type=F32)


def ring(k, n):
    return min(k % n, n - k % n)


def add_up(ref, n):
    total = ref[0].astype(F32)
    for k in range(1, n):
        total = total + ref[k].astype(F32)
    return total


def kernel(
    dims,
    pat_hbm, rhs_hbm, dinv_hbm, tiles_hbm, out,
    pat, rhs, dinv, tiles, load_sem,
    fwd, first, own, spread, part, red_f, red_a, part_b, red_b, back, gath, gath_f,
    send_sem, recv_sem,
):
    levels, rows, cols, rep, groups, gr, bs = dims
    nrhs = groups * gr
    slots = tiles.shape[1]
    nx, ny = cols // NY, NY
    me_r, me_c = lax.axis_index("row"), lax.axis_index("col")
    x, y = me_c // ny, lax.rem(me_c, ny)
    home = lax.rem(me_r, cols)
    blk_own = me_r // cols
    at_home = home == me_c
    home_x = home // ny
    is_owner = home_x == x
    barrier = pltpu.get_barrier_semaphore()

    def tell(r, c):
        pl.semaphore_signal(barrier, inc=1, device_id=(r, c), device_id_type=MESH)

    along = sorted(range(rows), key=lambda k: -ring(k // 2, rows // 2))
    plane = sorted(
        ((dx, dy) for dx in range(nx) for dy in range(ny)), key=lambda d: -ring(d[0], nx) - ring(d[1], ny)
    )
    turn = sorted(range(ny), key=lambda k: -ring(k, ny))

    def at_row(k):
        return lax.rem(me_r + k, rows)

    def at_plane(d):
        return lax.rem(x + d[0], nx) * ny + lax.rem(y + d[1], ny)

    for blk in range(rep):
        tell(me_c + cols * blk, me_c)

    loads = [
        pltpu.make_async_copy(rhs_hbm, rhs, load_sem.at[0]),
        pltpu.make_async_copy(dinv_hbm.at[0], dinv.at[0], load_sem.at[1]),
        pltpu.make_async_copy(pat_hbm, pat, load_sem.at[2]),
        pltpu.make_async_copy(tiles_hbm, tiles, load_sem.at[3]),
        pltpu.make_async_copy(dinv_hbm.at[pl.ds(1, levels - 1)], dinv.at[pl.ds(1, levels - 1)], load_sem.at[4]),
    ]
    for load in loads:
        load.start()

    @pl.when(is_owner)
    def _():
        for d in plane:
            tell(me_r, at_plane(d))

    drains = []

    def drain():
        while drains:
            drains.pop(0)()

    def send(src, dst, phase, r, c):
        pltpu.make_async_remote_copy(
            src_ref=src, dst_ref=dst, send_sem=send_sem.at[phase], recv_sem=recv_sem.at[phase],
            device_id=(r, c), device_id_type=MESH,
        ).start()

    def keep(src, dst, phase):
        pltpu.make_async_copy(src, dst, recv_sem.at[phase]).start()

    def arrived(ref, phase):
        pltpu.make_async_copy(ref, ref, recv_sem.at[phase]).wait()

    def sent(units, phase, when=None):
        def wait():
            left = units
            while left:
                n = min(left, rows)
                ref = red_b.at[0, pl.ds(0, n)]
                pltpu.make_async_copy(ref, ref, send_sem.at[phase]).wait()
                left -= n

        if when is None:
            drains.append(wait)
        else:
            drains.append(lambda: pl.when(when)(wait))

    loads[0].wait()
    loads[1].wait()
    phase = 0

    @pl.when(at_home)
    def _():
        first[...] = mm(rhs[0].reshape(nrhs, bs), dinv[0], NT).astype(BF16)
        pl.semaphore_wait(barrier, rows + groups)
        for k in along:
            if k:
                send(first, spread[0].at[blk_own], 0, at_row(k), me_c)
        keep(first, spread[0].at[blk_own], 0)

    @pl.when(jnp.logical_not(at_home))
    def _():
        pl.semaphore_wait(barrier, groups)

    @pl.when(is_owner)
    def _():
        fwd[0] = mm(rhs[0, y], dinv[0], NT)

    loads[2].wait()
    loads[3].wait()
    loads[4].wait()
    sent((rows - 1) * groups, 0, at_home)
    phase = 1

    for level in range(1, levels):
        sp = level - 1
        if level > 1:
            @pl.when(is_owner)
            def _(phase=phase, sp=sp):
                own[sp] = fwd[sp].astype(BF16)
                src, dst = own.at[sp], spread[sp].at[blk_own, y]
                for k in along:
                    if k:
                        send(src, dst, phase, at_row(k), home)

                @pl.when(at_home)
                def _():
                    keep(src, dst, phase)

                @pl.when(jnp.logical_not(at_home))
                def _():
                    send(src, dst, phase, me_r, home)

            drain()
            sent(rows - 1, phase, is_owner)
            sent(1, phase, jnp.logical_and(is_owner, jnp.logical_not(at_home)))
            phase += 1
        arrived(spread[sp], phase - 1)
        total = None
        for slot in range(slots):
            blk = pat[1, sp, slot] // cols
            source = spread[sp][blk].reshape(nrhs, bs)
            product = mm(source, tiles[sp, slot], NT)
            total = product if total is None else total + product
        part[sp] = total.astype(BF16).reshape(groups, gr, bs)
        if level < levels - 1:
            for k in turn:
                g = lax.rem(y + k, groups)
                src, dst = part.at[sp, g], red_f.at[sp, me_c]
                if k:
                    send(src, dst, phase, me_r, home_x * ny + g)
                else:
                    @pl.when(is_owner)
                    def _(src=src, dst=dst, phase=phase):
                        keep(src, dst, phase)

                    @pl.when(jnp.logical_not(is_owner))
                    def _(src=src, dst=dst, phase=phase):
                        send(src, dst, phase, me_r, home_x * ny + y)

            drain()
            sent(groups - 1, phase)
            sent(1, phase, jnp.logical_not(is_owner))

            @pl.when(is_owner)
            def _(sp=sp, level=level, phase=phase):
                arrived(red_f.at[sp], phase)
                current = rhs[level, y].astype(F32) - add_up(red_f.at[sp], cols)
                fwd[level] = mm(current.astype(BF16), dinv[level], NT)

        else:
            for d in plane:
                if d != (0, 0):
                    send(part.at[sp], red_a.at[me_c], phase, me_r, at_plane(d))
            keep(part.at[sp], red_a.at[me_c], phase)
            drain()
            sent((cols - 1) * groups, phase)
            arrived(red_a, phase)
            current = rhs[level].astype(F32) - add_up(red_a, cols)
            remainder = mm(current.astype(BF16).reshape(nrhs, bs), dinv[level], NT)
            solved = mm(remainder.astype(BF16), dinv[level], NN)
            out[level] = solved.reshape(groups, gr, bs)
            source = solved.astype(BF16)
        phase += 1

    for level in range(levels - 2, -1, -1):
        products = [mm(source, tiles[level, slot], NN) for slot in range(slots)]
        for blk in range(rep):
            total = None
            for slot in range(slots):
                hit = pat[1, level, slot] // cols == blk
                term = jnp.where(hit, products[slot], 0.0)
                total = term if total is None else total + term
            part_b[level, blk] = total.astype(BF16).reshape(groups, gr, bs)
        for k in turn:
            for blk in range(rep):
                g, row = lax.rem(y + k, groups), me_c + cols * blk
                src, dst = part_b.at[level, blk, g], red_b.at[level, me_r]
                if k:
                    send(src, dst, phase, row, x * ny + g)
                else:
                    @pl.when(row == me_r)
                    def _(src=src, dst=dst, phase=phase):
                        keep(src, dst, phase)

                    @pl.when(row != me_r)
                    def _(src=src, dst=dst, phase=phase, row=row):
                        send(src, dst, phase, row, me_c)

        drain()
        sent(rep * groups - 1, phase)
        sent(1, phase, jnp.logical_not(at_home))

        @pl.when(is_owner)
        def _(level=level, phase=phase):
            arrived(red_b.at[level], phase)
            remainder = fwd[level] - add_up(red_b.at[level], rows)
            solved = mm(remainder.astype(BF16), dinv[level], NN)
            back[level] = solved
            if level > 0:
                own[levels - 1 + level] = solved.astype(BF16)
                src, dst = own.at[levels - 1 + level], gath.at[level, y]
                for d in plane:
                    if d != (0, 0):
                        send(src, dst, phase + 1, me_r, at_plane(d))
                keep(src, dst, phase + 1)
            src, dst = back.at[level], gath_f.at[level, y]
            for d in plane:
                if d != (0, 0):
                    send(src, dst, phase + 2, me_r, at_plane(d))
            keep(src, dst, phase + 2)

        if level > 0:
            sent(cols - 1, phase + 1, is_owner)
        sent(2 * (cols - 1), phase + 2, is_owner)
        if level > 0:
            arrived(gath.at[level], phase + 1)
            source = gath[level].reshape(nrhs, bs)
        phase += 3

    drain()
    for level in range(levels - 2, -1, -1):
        arrived(gath_f.at[level], phase - 3 * level - 1)
        out[level] = gath_f[level]


def per_device(rhs, dinv, tiles, pattern):
    levels, _, nrhs, bs = rhs.shape
    rows, cols = lax.axis_size("row"), lax.axis_size("col")
    rep, groups = rows // cols, NY
    gr, slots = nrhs // groups, tiles.shape[2]
    pairs = levels - 1
    phases = 2 * pairs + 3 * pairs
    out = pl.pallas_call(
        functools.partial(kernel, (levels, rows, cols, rep, groups, gr, bs)),
        out_shape=jax.ShapeDtypeStruct((levels, groups, gr, bs), F32),
        in_specs=[pl.BlockSpec(memory_space=pl.ANY)] * 4,
        out_specs=pl.BlockSpec(memory_space=pltpu.VMEM),
        scratch_shapes=[
            pltpu.SMEM((2, pairs, slots), jnp.int32),
            pltpu.VMEM((levels, groups, gr, bs), BF16),
            pltpu.VMEM((levels, bs, bs), BF16),
            pltpu.VMEM((pairs, slots, bs, bs), BF16),
            pltpu.SemaphoreType.DMA((5,)),
            pltpu.VMEM((pairs, gr, bs), F32),
            pltpu.VMEM((nrhs, bs), BF16),
            pltpu.VMEM((2 * pairs, gr, bs), BF16),
            [pltpu.VMEM((rep, nrhs, bs), BF16)]
            + [pltpu.VMEM((rep, groups, gr, bs), BF16) for _ in range(pairs - 1)],
            pltpu.VMEM((pairs, groups, gr, bs), BF16),
            pltpu.VMEM((pairs, cols, gr, bs), BF16),
            pltpu.VMEM((cols, groups, gr, bs), BF16),
            pltpu.VMEM((pairs, rep, groups, gr, bs), BF16),
            pltpu.VMEM((pairs, rows, gr, bs), BF16),
            pltpu.VMEM((pairs, gr, bs), F32),
            pltpu.VMEM((pairs, groups, gr, bs), BF16),
            pltpu.VMEM((pairs, groups, gr, bs), F32),
            pltpu.SemaphoreType.DMA((phases,)),
            pltpu.SemaphoreType.DMA((phases,)),
        ],
        compiler_params=pltpu.CompilerParams(
            collective_id=0, has_side_effects=True
        ),
    )(
        pattern[:, :, 0, :],
        rhs.reshape(levels, groups, gr, bs),
        dinv.reshape(levels, bs, bs),
        tiles.reshape(pairs, slots, bs, bs),
    )
    return out.reshape(levels, 1, nrhs, bs)


def solution(mesh):
    in_specs = (
        P(None, "row", None, None),
        P(None, "row", None, None),
        P(None, "row", "col", None, None),
        P(None, None, "row", "col"),
    )
    return jax.shard_map(
        per_device, mesh=mesh, in_specs=in_specs, out_specs=P(None, "row", None, None), check_vma=False
    )
```

```python
import functools

import jax
import jax.numpy as jnp
from jax import lax
from jax.experimental import pallas as pl
from jax.experimental.pallas import tpu as pltpu
from jax.sharding import PartitionSpec as P

MESH = pl.DeviceIdType.MESH
BF16, F32 = jnp.bfloat16, jnp.float32
NT = (((1,), (1,)), ((), ()))
NN = (((1,), (0,)), ((), ()))
NY = 4


def mm(a, b, dims):
    return lax.dot_general(a, b, dims, preferred_element_type=F32)


def ring(k, n):
    return min(k % n, n - k % n)


def add_up(ref, n):
    total = ref[0].astype(F32)
    for k in range(1, n):
        total = total + ref[k].astype(F32)
    return total


def kernel(
    dims,
    pat_hbm, rhs_hbm, dinv_hbm, tiles_hbm, out,
    pat, rhs, dinv, tiles, load_sem,
    fwd, first, own, spread, part, red_f, red_a, part_b, red_b, back, gath, gath_f,
    send_sem, recv_sem,
):
    levels, rows, cols, rep, groups, gr, bs = dims
    nrhs = groups * gr
    slots = tiles.shape[1]
    nx, ny = cols // NY, NY
    me_r, me_c = lax.axis_index("row"), lax.axis_index("col")
    x, y = me_c // ny, lax.rem(me_c, ny)
    home = lax.rem(me_r, cols)
    blk_own = me_r // cols
    at_home = home == me_c
    home_y = lax.rem(home, ny)
    is_owner = home_y == y
    barrier = pltpu.get_barrier_semaphore()

    def tell(r, c):
        pl.semaphore_signal(barrier, inc=1, device_id=(r, c), device_id_type=MESH)

    along = sorted(range(rows), key=lambda k: -ring(k // 2, rows // 2))
    plane = sorted(
        ((dx, dy) for dx in range(nx) for dy in range(ny)), key=lambda d: -ring(d[0], nx) - ring(d[1], ny)
    )
    turn = sorted(range(nx), key=lambda k: -ring(k, nx))

    def at_row(k):
        return lax.rem(me_r + k, rows)

    def at_plane(d):
        return lax.rem(x + d[0], nx) * ny + lax.rem(y + d[1], ny)

    for blk in range(rep):
        tell(me_c + cols * blk, me_c)

    loads = [
        pltpu.make_async_copy(rhs_hbm, rhs, load_sem.at[0]),
        pltpu.make_async_copy(dinv_hbm.at[0], dinv.at[0], load_sem.at[1]),
        pltpu.make_async_copy(pat_hbm, pat, load_sem.at[2]),
        pltpu.make_async_copy(tiles_hbm, tiles, load_sem.at[3]),
        pltpu.make_async_copy(dinv_hbm.at[pl.ds(1, levels - 1)], dinv.at[pl.ds(1, levels - 1)], load_sem.at[4]),
    ]
    for load in loads:
        load.start()

    @pl.when(is_owner)
    def _():
        for d in plane:
            tell(me_r, at_plane(d))

    drains = []

    def drain():
        while drains:
            drains.pop(0)()

    def send(src, dst, phase, r, c):
        pltpu.make_async_remote_copy(
            src_ref=src, dst_ref=dst, send_sem=send_sem.at[phase], recv_sem=recv_sem.at[phase],
            device_id=(r, c), device_id_type=MESH,
        ).start()

    def keep(src, dst, phase):
        pltpu.make_async_copy(src, dst, recv_sem.at[phase]).start()

    def arrived(ref, phase):
        pltpu.make_async_copy(ref, ref, recv_sem.at[phase]).wait()

    def sent(units, phase, when=None):
        def wait():
            left = units
            while left:
                n = min(left, rows)
                ref = red_b.at[0, pl.ds(0, n)]
                pltpu.make_async_copy(ref, ref, send_sem.at[phase]).wait()
                left -= n

        if when is None:
            drains.append(wait)
        else:
            drains.append(lambda: pl.when(when)(wait))

    loads[0].wait()
    loads[1].wait()
    phase = 0

    @pl.when(at_home)
    def _():
        first[...] = mm(rhs[0].reshape(nrhs, bs), dinv[0], NT).astype(BF16)
        pl.semaphore_wait(barrier, rows + groups)
        for k in along:
            if k:
                send(first, spread[0].at[blk_own], 0, at_row(k), me_c)
        keep(first, spread[0].at[blk_own], 0)

    @pl.when(jnp.logical_not(at_home))
    def _():
        pl.semaphore_wait(barrier, groups)

    @pl.when(is_owner)
    def _():
        fwd[0] = mm(rhs[0, x], dinv[0], NT)

    loads[2].wait()
    loads[3].wait()
    loads[4].wait()
    sent((rows - 1) * groups, 0, at_home)
    phase = 1

    for level in range(1, levels):
        sp = level - 1
        if level > 1:
            @pl.when(is_owner)
            def _(phase=phase, sp=sp):
                own[sp] = fwd[sp].astype(BF16)
                src, dst = own.at[sp], spread[sp].at[blk_own, x]
                for k in along:
                    if k:
                        send(src, dst, phase, at_row(k), home)

                @pl.when(at_home)
                def _():
                    keep(src, dst, phase)

                @pl.when(jnp.logical_not(at_home))
                def _():
                    send(src, dst, phase, me_r, home)

            drain()
            sent(rows - 1, phase, is_owner)
            sent(1, phase, jnp.logical_and(is_owner, jnp.logical_not(at_home)))
            phase += 1
        arrived(spread[sp], phase - 1)
        total = None
        for slot in range(slots):
            blk = pat[1, sp, slot] // cols
            source = spread[sp][blk].reshape(nrhs, bs)
            product = mm(source, tiles[sp, slot], NT)
            total = product if total is None else total + product
        part[sp] = total.astype(BF16).reshape(groups, gr, bs)
        if level < levels - 1:
            for k in turn:
                g = lax.rem(x + k, groups)
                src, dst = part.at[sp, g], red_f.at[sp, me_c]
                if k:
                    send(src, dst, phase, me_r, g * ny + home_y)
                else:
                    @pl.when(is_owner)
                    def _(src=src, dst=dst, phase=phase):
                        keep(src, dst, phase)

                    @pl.when(jnp.logical_not(is_owner))
                    def _(src=src, dst=dst, phase=phase):
                        send(src, dst, phase, me_r, x * ny + home_y)

            drain()
            sent(groups - 1, phase)
            sent(1, phase, jnp.logical_not(is_owner))

            @pl.when(is_owner)
            def _(sp=sp, level=level, phase=phase):
                arrived(red_f.at[sp], phase)
                current = rhs[level, x].astype(F32) - add_up(red_f.at[sp], cols)
                fwd[level] = mm(current.astype(BF16), dinv[level], NT)

        else:
            for d in plane:
                if d != (0, 0):
                    send(part.at[sp], red_a.at[me_c], phase, me_r, at_plane(d))
            keep(part.at[sp], red_a.at[me_c], phase)
            drain()
            sent((cols - 1) * groups, phase)
            arrived(red_a, phase)
            current = rhs[level].astype(F32) - add_up(red_a, cols)
            remainder = mm(current.astype(BF16).reshape(nrhs, bs), dinv[level], NT)
            solved = mm(remainder.astype(BF16), dinv[level], NN)
            out[level] = solved.reshape(groups, gr, bs)
            source = solved.astype(BF16)
        phase += 1

    def gather_f(level, phase):
        src, dst = back.at[level], gath_f.at[level, x]
        for d in plane:
            if d != (0, 0):
                send(src, dst, phase, me_r, at_plane(d))
        keep(src, dst, phase)

    for level in range(levels - 2, -1, -1):
        products = [mm(source, tiles[level, slot], NN) for slot in range(slots)]
        for blk in range(rep):
            total = None
            for slot in range(slots):
                hit = pat[1, level, slot] // cols == blk
                term = jnp.where(hit, products[slot], 0.0)
                total = term if total is None else total + term
            part_b[level, blk] = total.astype(BF16).reshape(groups, gr, bs)
        for k in turn:
            for blk in range(rep):
                g, row = lax.rem(x + k, groups), me_c + cols * blk
                src, dst = part_b.at[level, blk, g], red_b.at[level, me_r]
                if k:
                    send(src, dst, phase, row, g * ny + y)
                else:
                    @pl.when(row == me_r)
                    def _(src=src, dst=dst, phase=phase):
                        keep(src, dst, phase)

                    @pl.when(row != me_r)
                    def _(src=src, dst=dst, phase=phase, row=row):
                        send(src, dst, phase, row, me_c)

        if level < levels - 2:
            @pl.when(is_owner)
            def _(level=level, phase=phase):
                gather_f(level + 1, phase - 1)

        drain()
        if level < levels - 2:
            sent(2 * (cols - 1), phase - 1, is_owner)
        sent(rep * groups - 1, phase)
        sent(1, phase, jnp.logical_not(at_home))

        @pl.when(is_owner)
        def _(level=level, phase=phase):
            arrived(red_b.at[level], phase)
            remainder = fwd[level] - add_up(red_b.at[level], rows)
            solved = mm(remainder.astype(BF16), dinv[level], NN)
            back[level] = solved
            if level > 0:
                own[levels - 1 + level] = solved.astype(BF16)
                src, dst = own.at[levels - 1 + level], gath.at[level, x]
                for d in plane:
                    if d != (0, 0):
                        send(src, dst, phase + 1, me_r, at_plane(d))
                keep(src, dst, phase + 1)
            if level == 0:
                gather_f(0, phase + 2)

        if level > 0:
            sent(cols - 1, phase + 1, is_owner)
        if level == 0:
            sent(2 * (cols - 1), phase + 2, is_owner)
        if level > 0:
            arrived(gath.at[level], phase + 1)
            source = gath[level].reshape(nrhs, bs)
        phase += 3

    drain()
    for level in range(levels - 2, -1, -1):
        arrived(gath_f.at[level], phase - 3 * level - 1)
        out[level] = gath_f[level]


def per_device(rhs, dinv, tiles, pattern):
    levels, _, nrhs, bs = rhs.shape
    rows, cols = lax.axis_size("row"), lax.axis_size("col")
    rep, groups = rows // cols, cols // NY
    gr, slots = nrhs // groups, tiles.shape[2]
    pairs = levels - 1
    phases = 2 * pairs + 3 * pairs
    out = pl.pallas_call(
        functools.partial(kernel, (levels, rows, cols, rep, groups, gr, bs)),
        out_shape=jax.ShapeDtypeStruct((levels, groups, gr, bs), F32),
        in_specs=[pl.BlockSpec(memory_space=pl.ANY)] * 4,
        out_specs=pl.BlockSpec(memory_space=pltpu.VMEM),
        scratch_shapes=[
            pltpu.SMEM((2, pairs, slots), jnp.int32),
            pltpu.VMEM((levels, groups, gr, bs), BF16),
            pltpu.VMEM((levels, bs, bs), BF16),
            pltpu.VMEM((pairs, slots, bs, bs), BF16),
            pltpu.SemaphoreType.DMA((5,)),
            pltpu.VMEM((pairs, gr, bs), F32),
            pltpu.VMEM((nrhs, bs), BF16),
            pltpu.VMEM((2 * pairs, gr, bs), BF16),
            [pltpu.VMEM((rep, nrhs, bs), BF16)]
            + [pltpu.VMEM((rep, groups, gr, bs), BF16) for _ in range(pairs - 1)],
            pltpu.VMEM((pairs, groups, gr, bs), BF16),
            pltpu.VMEM((pairs, cols, gr, bs), BF16),
            pltpu.VMEM((cols, groups, gr, bs), BF16),
            pltpu.VMEM((pairs, rep, groups, gr, bs), BF16),
            pltpu.VMEM((pairs, rows, gr, bs), BF16),
            pltpu.VMEM((pairs, gr, bs), F32),
            pltpu.VMEM((pairs, groups, gr, bs), BF16),
            pltpu.VMEM((pairs, groups, gr, bs), F32),
            pltpu.SemaphoreType.DMA((phases,)),
            pltpu.SemaphoreType.DMA((phases,)),
        ],
        compiler_params=pltpu.CompilerParams(
            collective_id=0, has_side_effects=True, vmem_limit_bytes=16 * 2**20
        ),
    )(
        *[
            pltpu.with_memory_space_constraint(a, pltpu.HBM)
            for a in (
                pattern[:, :, 0, :],
                rhs.reshape(levels, groups, gr, bs),
                dinv.reshape(levels, bs, bs),
                tiles.reshape(pairs, slots, bs, bs),
            )
        ]
    )
    return out.reshape(levels, 1, nrhs, bs)


def solution(mesh):
    in_specs = (
        P(None, "row", None, None),
        P(None, "row", None, None),
        P(None, "row", "col", None, None),
        P(None, None, "row", "col"),
    )
    return jax.shard_map(
        per_device, mesh=mesh, in_specs=in_specs, out_specs=P(None, "row", None, None), check_vma=False
    )
```

```python
import functools

import jax
import jax.numpy as jnp
from jax import lax
from jax.experimental import pallas as pl
from jax.experimental.pallas import tpu as pltpu
from jax.sharding import PartitionSpec as P

MESH = pl.DeviceIdType.MESH
BF16, F32 = jnp.bfloat16, jnp.float32
NT = (((1,), (1,)), ((), ()))
NN = (((1,), (0,)), ((), ()))
NY = 4
GROUPS = 1
PARTS = 2


def mm(a, b, dims):
    return lax.dot_general(a, b, dims, preferred_element_type=F32)


def ring(k, n):
    return min(k % n, n - k % n)


def add_up(ref, n):
    total = ref[0].astype(F32)
    for k in range(1, n):
        total = total + ref[k].astype(F32)
    return total


def kernel(
    dims,
    pat_hbm, rhs_hbm, dinv_hbm, tiles_hbm, out,
    pat, rhs, dinv, tiles, load_sem,
    fwd, first, own, spread, part, red_f, red_a, part_b, red_b, gath,
    send_sem, recv_sem,
):
    levels, rows, cols, rep, parts, groups, gr, bs = dims
    nrhs = groups * gr
    slots = tiles.shape[1]
    nx, ny = cols // NY, NY
    me_r, me_c = lax.axis_index("row"), lax.axis_index("col")
    x, y = me_c // ny, lax.rem(me_c, ny)
    home = lax.rem(me_r, cols)
    blk_own = me_r // cols
    at_home = home == me_c
    home_x, home_y = home // ny, lax.rem(home, ny)
    g_own = lax.rem(x + nx - home_x, nx)
    is_owner = jnp.logical_and(home_y == y, g_own < groups)
    g_own = jnp.minimum(g_own, groups - 1)
    barrier = pltpu.get_barrier_semaphore()

    def tell(r, c):
        pl.semaphore_signal(barrier, inc=1, device_id=(r, c), device_id_type=MESH)

    along = sorted(range(rows), key=lambda k: -ring(k // 2, rows // 2))
    plane = sorted(
        ((dx, dy) for dx in range(nx) for dy in range(ny)), key=lambda d: -ring(d[0], nx) - ring(d[1], ny)
    )

    def at_row(k):
        return lax.rem(me_r + k, rows)

    def at_plane(d):
        return lax.rem(x + d[0], nx) * ny + lax.rem(y + d[1], ny)

    for blk in range(rep):
        tell(me_c + cols * blk, me_c)

    loads = [
        pltpu.make_async_copy(rhs_hbm, rhs, load_sem.at[0]),
        pltpu.make_async_copy(dinv_hbm.at[0], dinv.at[0], load_sem.at[1]),
        pltpu.make_async_copy(pat_hbm, pat, load_sem.at[2]),
        pltpu.make_async_copy(tiles_hbm, tiles, load_sem.at[3]),
        pltpu.make_async_copy(dinv_hbm.at[pl.ds(1, levels - 1)], dinv.at[pl.ds(1, levels - 1)], load_sem.at[4]),
    ]
    for load in loads:
        load.start()

    @pl.when(is_owner)
    def _():
        for d in plane:
            tell(me_r, at_plane(d))

    waits = []

    def drain(lag):
        while len(waits) > lag:
            for wait in waits.pop(0):
                wait()

    def send(src, dst, h, phase, r, c):
        pltpu.make_async_remote_copy(
            src_ref=src, dst_ref=dst, send_sem=send_sem.at[h, phase], recv_sem=recv_sem.at[h, phase],
            device_id=(r, c), device_id_type=MESH,
        ).start()

    def keep(src, dst, h, phase):
        pltpu.make_async_copy(src, dst, recv_sem.at[h, phase]).start()

    def arrived(ref, h, phase):
        pltpu.make_async_copy(ref, ref, recv_sem.at[h, phase]).wait()

    def sent(phase, *pieces):
        def wait(h, units, when):
            def act():
                left = units
                while left:
                    n = min(left, rows)
                    ref = red_b.at[0, 0, pl.ds(0, n)]
                    pltpu.make_async_copy(ref, ref, send_sem.at[h, phase]).wait()
                    left -= n

            return act if when is None else lambda: pl.when(when)(act)

        waits.append([wait(h, *piece) for h in range(parts) for piece in pieces])

    loads[0].wait()
    loads[1].wait()
    phase = 0

    @pl.when(at_home)
    def _():
        solved = mm(rhs[0].reshape(parts * nrhs, bs), dinv[0], NT)
        first[...] = solved.astype(BF16).reshape(parts, nrhs, bs)
        pl.semaphore_wait(barrier, rows + groups)
        for h in range(parts):
            src, dst = first.at[h], spread[0][h].at[blk_own]
            for k in along:
                if k:
                    send(src, dst, h, 0, at_row(k), me_c)
            keep(src, dst, h, 0)

    @pl.when(jnp.logical_not(at_home))
    def _():
        pl.semaphore_wait(barrier, groups)

    @pl.when(is_owner)
    def _():
        for h in range(parts):
            fwd[h, 0] = mm(rhs[0, h, g_own], dinv[0], NT)

    loads[2].wait()
    loads[3].wait()
    loads[4].wait()
    sent(0, ((rows - 1) * groups, at_home))
    phase = 1

    for level in range(1, levels):
        sp = level - 1
        if level > 1:
            @pl.when(is_owner)
            def _(phase=phase, sp=sp):
                for h in range(parts):
                    arrived(red_f.at[h, sp - 1], h, phase - 1)
                    current = rhs[sp, h, g_own].astype(F32) - add_up(red_f.at[h, sp - 1], cols)
                    solved = mm(current.astype(BF16), dinv[sp], NT)
                    fwd[h, sp] = solved
                    own[h, sp] = solved.astype(BF16)
                    src, dst = own.at[h, sp], spread[sp][h].at[blk_own, g_own]
                    for k in along:
                        if k:
                            send(src, dst, h, phase, at_row(k), home)

                    @pl.when(at_home)
                    def _(src=src, dst=dst, h=h):
                        keep(src, dst, h, phase)

                    @pl.when(jnp.logical_not(at_home))
                    def _(src=src, dst=dst, h=h):
                        send(src, dst, h, phase, me_r, home)

            sent(phase, (rows - 1, is_owner), (1, jnp.logical_and(is_owner, jnp.logical_not(at_home))))
            drain(2)
            phase += 1
        for h in range(parts):
            arrived(spread[sp][h], h, phase - 1)
            total = None
            for slot in range(slots):
                blk = pat[1, sp, slot] // cols
                source = spread[sp][h][blk].reshape(nrhs, bs)
                product = mm(source, tiles[sp, slot], NT)
                total = product if total is None else total + product
            part[h, sp] = total.astype(BF16).reshape(groups, gr, bs)
            if level < levels - 1:
                for g in range(groups):
                    src, dst = part.at[h, sp, g], red_f.at[h, sp, me_c]
                    col = lax.rem(home_x + g, nx) * ny + home_y

                    @pl.when(col == me_c)
                    def _(src=src, dst=dst, phase=phase, h=h):
                        keep(src, dst, h, phase)

                    @pl.when(col != me_c)
                    def _(src=src, dst=dst, phase=phase, h=h, col=col):
                        send(src, dst, h, phase, me_r, col)

            else:
                for d in plane:
                    if d != (0, 0):
                        send(part.at[h, sp], red_a.at[h, me_c], h, phase, me_r, at_plane(d))
                keep(part.at[h, sp], red_a.at[h, me_c], h, phase)

        if level < levels - 1:
            sent(phase, (groups - 1, None), (1, jnp.logical_not(is_owner)))
        else:
            sent(phase, ((cols - 1) * groups, None))
        drain(2)
        phase += 1

    for level in range(levels - 2, -1, -1):
        for h in range(parts):
            if level == levels - 2:
                arrived(red_a.at[h], h, phase - 1)
                current = rhs[level + 1, h].astype(F32) - add_up(red_a.at[h], cols)
                remainder = mm(current.astype(BF16).reshape(nrhs, bs), dinv[level + 1], NT)
                solved = mm(remainder.astype(BF16), dinv[level + 1], NN)
                out[level + 1, h] = solved.reshape(groups, gr, bs)
                source = solved.astype(BF16)
            else:
                arrived(gath.at[h, level + 1], h, phase - 1)
                source = gath[h, level + 1].reshape(nrhs, bs)
            products = [mm(source, tiles[level, slot], NN) for slot in range(slots)]
            for blk in range(rep):
                total = None
                for slot in range(slots):
                    hit = pat[1, level, slot] // cols == blk
                    term = jnp.where(hit, products[slot], 0.0)
                    total = term if total is None else total + term
                part_b[h, level, blk] = total.astype(BF16).reshape(groups, gr, bs)
            for g in range(groups - 1, -1, -1):
                for blk in range(rep):
                    row = me_c + cols * blk
                    src, dst = part_b.at[h, level, blk, g], red_b.at[h, level, me_r]
                    if g:
                        send(src, dst, h, phase, row, lax.rem(x + g, nx) * ny + y)
                    else:
                        @pl.when(row == me_r)
                        def _(src=src, dst=dst, phase=phase, h=h):
                            keep(src, dst, h, phase)

                        @pl.when(row != me_r)
                        def _(src=src, dst=dst, phase=phase, row=row, h=h):
                            send(src, dst, h, phase, row, me_c)

            if level < levels - 2:
                out[level + 1, h] = gath[h, level + 1].astype(F32)

        sent(phase, (rep * groups - 1, None), (1, jnp.logical_not(at_home)))
        drain(2)

        @pl.when(is_owner)
        def _(level=level, phase=phase):
            for h in range(parts):
                arrived(red_b.at[h, level], h, phase)
                remainder = fwd[h, level] - add_up(red_b.at[h, level], rows)
                solved = mm(remainder.astype(BF16), dinv[level], NN)
                own[h, levels - 1 + level] = solved.astype(BF16)
                src, dst = own.at[h, levels - 1 + level], gath.at[h, level, g_own]
                for d in plane:
                    if d != (0, 0):
                        send(src, dst, h, phase + 1, me_r, at_plane(d))
                keep(src, dst, h, phase + 1)

        sent(phase + 1, (cols - 1, is_owner))
        drain(1 if level == 0 else 2)
        phase += 2

    for h in range(parts):
        arrived(gath.at[h, 0], h, phase - 1)
        out[0, h] = gath[h, 0].astype(F32)
    drain(0)


def per_device(rhs, dinv, tiles, pattern):
    levels, _, nrhs, bs = rhs.shape
    rows, cols = lax.axis_size("row"), lax.axis_size("col")
    rep, parts, groups = rows // cols, PARTS, GROUPS
    gr, slots = nrhs // (parts * groups), tiles.shape[2]
    pairs = levels - 1
    phases = 2 * pairs + 2 * pairs
    out = pl.pallas_call(
        functools.partial(kernel, (levels, rows, cols, rep, parts, groups, gr, bs)),
        out_shape=jax.ShapeDtypeStruct((levels, parts, groups, gr, bs), F32),
        in_specs=[pl.BlockSpec(memory_space=pl.ANY)] * 4,
        out_specs=pl.BlockSpec(memory_space=pltpu.VMEM),
        scratch_shapes=[
            pltpu.SMEM((2, pairs, slots), jnp.int32),
            pltpu.VMEM((levels, parts, groups, gr, bs), BF16),
            pltpu.VMEM((levels, bs, bs), BF16),
            pltpu.VMEM((pairs, slots, bs, bs), BF16),
            pltpu.SemaphoreType.DMA((5,)),
            pltpu.VMEM((parts, pairs, gr, bs), F32),
            pltpu.VMEM((parts, groups * gr, bs), BF16),
            pltpu.VMEM((parts, 2 * pairs, gr, bs), BF16),
            [[pltpu.VMEM((rep, groups * gr, bs), BF16) for _ in range(parts)]]
            + [[pltpu.VMEM((rep, groups, gr, bs), BF16) for _ in range(parts)] for _ in range(pairs - 1)],
            pltpu.VMEM((parts, pairs, groups, gr, bs), BF16),
            pltpu.VMEM((parts, pairs, cols, gr, bs), BF16),
            pltpu.VMEM((parts, cols, groups, gr, bs), BF16),
            pltpu.VMEM((parts, pairs, rep, groups, gr, bs), BF16),
            pltpu.VMEM((parts, pairs, rows, gr, bs), BF16),
            pltpu.VMEM((parts, pairs, groups, gr, bs), BF16),
            pltpu.SemaphoreType.DMA((parts, phases)),
            pltpu.SemaphoreType.DMA((parts, phases)),
        ],
        compiler_params=pltpu.CompilerParams(
            collective_id=0, has_side_effects=True, vmem_limit_bytes=16 * 2**20
        ),
    )(
        *[
            pltpu.with_memory_space_constraint(a, pltpu.HBM)
            for a in (
                pattern[:, :, 0, :],
                rhs.reshape(levels, parts, groups, gr, bs),
                dinv.reshape(levels, bs, bs),
                tiles.reshape(pairs, slots, bs, bs),
            )
        ]
    )
    return out.reshape(levels, 1, nrhs, bs)


def solution(mesh):
    in_specs = (
        P(None, "row", None, None),
        P(None, "row", None, None),
        P(None, "row", "col", None, None),
        P(None, None, "row", "col"),
    )
    return jax.shard_map(
        per_device, mesh=mesh, in_specs=in_specs, out_specs=P(None, "row", None, None), check_vma=False
    )
```

```python
import functools

import jax
import jax.numpy as jnp
from jax import lax
from jax.experimental import pallas as pl
from jax.experimental.pallas import tpu as pltpu
from jax.sharding import PartitionSpec as P

MESH = pl.DeviceIdType.MESH
BF16, F32 = jnp.bfloat16, jnp.float32
NT = (((1,), (1,)), ((), ()))
NN = (((1,), (0,)), ((), ()))
NY = 4
GROUPS = 1
PARTS = 4


def mm(a, b, dims):
    return lax.dot_general(a, b, dims, preferred_element_type=F32)


def ring(k, n):
    return min(k % n, n - k % n)


def add_up(ref, n):
    total = ref[0].astype(F32)
    for k in range(1, n):
        total = total + ref[k].astype(F32)
    return total


def kernel(
    dims,
    pat_hbm, rhs_hbm, dinv_hbm, tiles_hbm, out,
    pat, rhs, dinv, tiles, load_sem,
    fwd, first, own, spread, part, red_f, red_a, part_b, red_b, gath,
    send_sem, recv_sem,
):
    levels, rows, cols, rep, parts, groups, gr, bs = dims
    nrhs = groups * gr
    slots = tiles.shape[1]
    nx, ny = cols // NY, NY
    me_r, me_c = lax.axis_index("row"), lax.axis_index("col")
    x, y = me_c // ny, lax.rem(me_c, ny)
    home = lax.rem(me_r, cols)
    blk_own = me_r // cols
    at_home = home == me_c
    home_x, home_y = home // ny, lax.rem(home, ny)
    g_own = lax.rem(x + nx - home_x, nx)
    is_owner = jnp.logical_and(home_y == y, g_own < groups)
    g_own = jnp.minimum(g_own, groups - 1)
    barrier = pltpu.get_barrier_semaphore()

    def tell(r, c):
        pl.semaphore_signal(barrier, inc=1, device_id=(r, c), device_id_type=MESH)

    along = sorted(range(rows), key=lambda k: -ring(k // 2, rows // 2))
    plane = sorted(
        ((dx, dy) for dx in range(nx) for dy in range(ny)), key=lambda d: -ring(d[0], nx) - ring(d[1], ny)
    )

    def at_row(k):
        return lax.rem(me_r + k, rows)

    def at_plane(d):
        return lax.rem(x + d[0], nx) * ny + lax.rem(y + d[1], ny)

    for blk in range(rep):
        tell(me_c + cols * blk, me_c)

    loads = [
        pltpu.make_async_copy(rhs_hbm, rhs, load_sem.at[0]),
        pltpu.make_async_copy(dinv_hbm.at[0], dinv.at[0], load_sem.at[1]),
        pltpu.make_async_copy(pat_hbm, pat, load_sem.at[2]),
        pltpu.make_async_copy(tiles_hbm, tiles, load_sem.at[3]),
        pltpu.make_async_copy(dinv_hbm.at[pl.ds(1, levels - 1)], dinv.at[pl.ds(1, levels - 1)], load_sem.at[4]),
    ]
    for load in loads:
        load.start()

    @pl.when(is_owner)
    def _():
        for d in plane:
            tell(me_r, at_plane(d))

    waits = []

    def drain(lag):
        while len(waits) > lag:
            for wait in waits.pop(0):
                wait()

    def send(src, dst, h, phase, r, c):
        pltpu.make_async_remote_copy(
            src_ref=src, dst_ref=dst, send_sem=send_sem.at[h, phase], recv_sem=recv_sem.at[h, phase],
            device_id=(r, c), device_id_type=MESH,
        ).start()

    def keep(src, dst, h, phase):
        pltpu.make_async_copy(src, dst, recv_sem.at[h, phase]).start()

    def arrived(ref, h, phase):
        pltpu.make_async_copy(ref, ref, recv_sem.at[h, phase]).wait()

    def sent(phase, *pieces):
        def wait(h, units, when):
            def act():
                left = units
                while left:
                    n = min(left, rows)
                    ref = red_b.at[0, 0, pl.ds(0, n)]
                    pltpu.make_async_copy(ref, ref, send_sem.at[h, phase]).wait()
                    left -= n

            return act if when is None else lambda: pl.when(when)(act)

        waits.append([wait(h, *piece) for h in range(parts) for piece in pieces])

    loads[0].wait()
    loads[1].wait()
    phase = 0

    @pl.when(at_home)
    def _():
        solved = mm(rhs[0].reshape(parts * nrhs, bs), dinv[0], NT)
        first[...] = solved.astype(BF16).reshape(parts, nrhs, bs)
        pl.semaphore_wait(barrier, rows + groups)
        for h in range(parts):
            src, dst = first.at[h], spread[0][h].at[blk_own]
            for k in along:
                if k:
                    send(src, dst, h, 0, at_row(k), me_c)
            keep(src, dst, h, 0)

    @pl.when(jnp.logical_not(at_home))
    def _():
        pl.semaphore_wait(barrier, groups)

    @pl.when(is_owner)
    def _():
        for h in range(parts):
            fwd[h, 0] = mm(rhs[0, h, g_own], dinv[0], NT)

    loads[2].wait()
    loads[3].wait()
    loads[4].wait()
    sent(0, ((rows - 1) * groups, at_home))
    phase = 1

    for level in range(1, levels):
        sp = level - 1
        if level > 1:
            @pl.when(is_owner)
            def _(phase=phase, sp=sp):
                for h in range(parts):
                    arrived(red_f.at[h, sp - 1], h, phase - 1)
                    current = rhs[sp, h, g_own].astype(F32) - add_up(red_f.at[h, sp - 1], cols)
                    solved = mm(current.astype(BF16), dinv[sp], NT)
                    fwd[h, sp] = solved
                    own[h, sp] = solved.astype(BF16)
                    src, dst = own.at[h, sp], spread[sp][h].at[blk_own, g_own]
                    for k in along:
                        if k:
                            send(src, dst, h, phase, at_row(k), home)

                    @pl.when(at_home)
                    def _(src=src, dst=dst, h=h):
                        keep(src, dst, h, phase)

                    @pl.when(jnp.logical_not(at_home))
                    def _(src=src, dst=dst, h=h):
                        send(src, dst, h, phase, me_r, home)

            sent(phase, (rows - 1, is_owner), (1, jnp.logical_and(is_owner, jnp.logical_not(at_home))))
            drain(2)
            phase += 1
        for h in range(parts):
            arrived(spread[sp][h], h, phase - 1)
            total = None
            for slot in range(slots):
                blk = pat[1, sp, slot] // cols
                source = spread[sp][h][blk].reshape(nrhs, bs)
                product = mm(source, tiles[sp, slot], NT)
                total = product if total is None else total + product
            part[h, sp] = total.astype(BF16).reshape(groups, gr, bs)
            if level < levels - 1:
                for g in range(groups):
                    src, dst = part.at[h, sp, g], red_f.at[h, sp, me_c]
                    col = lax.rem(home_x + g, nx) * ny + home_y

                    @pl.when(col == me_c)
                    def _(src=src, dst=dst, phase=phase, h=h):
                        keep(src, dst, h, phase)

                    @pl.when(col != me_c)
                    def _(src=src, dst=dst, phase=phase, h=h, col=col):
                        send(src, dst, h, phase, me_r, col)

            else:
                for d in plane:
                    if d != (0, 0):
                        send(part.at[h, sp], red_a.at[h, me_c], h, phase, me_r, at_plane(d))
                keep(part.at[h, sp], red_a.at[h, me_c], h, phase)

        if level < levels - 1:
            sent(phase, (groups - 1, None), (1, jnp.logical_not(is_owner)))
        else:
            sent(phase, ((cols - 1) * groups, None))
        drain(2)
        phase += 1

    for level in range(levels - 2, -1, -1):
        for h in range(parts):
            if level == levels - 2:
                arrived(red_a.at[h], h, phase - 1)
                current = rhs[level + 1, h].astype(F32) - add_up(red_a.at[h], cols)
                remainder = mm(current.astype(BF16).reshape(nrhs, bs), dinv[level + 1], NT)
                solved = mm(remainder.astype(BF16), dinv[level + 1], NN)
                out[level + 1, h] = solved.reshape(groups, gr, bs)
                source = solved.astype(BF16)
            else:
                arrived(gath.at[h, level + 1], h, phase - 1)
                source = gath[h, level + 1].reshape(nrhs, bs)
            products = [mm(source, tiles[level, slot], NN) for slot in range(slots)]
            for blk in range(rep):
                total = None
                for slot in range(slots):
                    hit = pat[1, level, slot] // cols == blk
                    term = jnp.where(hit, products[slot], 0.0)
                    total = term if total is None else total + term
                part_b[h, level, blk] = total.astype(BF16).reshape(groups, gr, bs)
            for g in range(groups - 1, -1, -1):
                for blk in range(rep):
                    row = me_c + cols * blk
                    src, dst = part_b.at[h, level, blk, g], red_b.at[h, level, me_r]
                    if g:
                        send(src, dst, h, phase, row, lax.rem(x + g, nx) * ny + y)
                    else:
                        @pl.when(row == me_r)
                        def _(src=src, dst=dst, phase=phase, h=h):
                            keep(src, dst, h, phase)

                        @pl.when(row != me_r)
                        def _(src=src, dst=dst, phase=phase, row=row, h=h):
                            send(src, dst, h, phase, row, me_c)

            if level < levels - 2:
                out[level + 1, h] = gath[h, level + 1].astype(F32)

        sent(phase, (rep * groups - 1, None), (1, jnp.logical_not(at_home)))
        drain(2)

        @pl.when(is_owner)
        def _(level=level, phase=phase):
            for h in range(parts):
                arrived(red_b.at[h, level], h, phase)
                remainder = fwd[h, level] - add_up(red_b.at[h, level], rows)
                solved = mm(remainder.astype(BF16), dinv[level], NN)
                own[h, levels - 1 + level] = solved.astype(BF16)
                src, dst = own.at[h, levels - 1 + level], gath.at[h, level, g_own]
                for d in plane:
                    if d != (0, 0):
                        send(src, dst, h, phase + 1, me_r, at_plane(d))
                keep(src, dst, h, phase + 1)

        sent(phase + 1, (cols - 1, is_owner))
        drain(1 if level == 0 else 2)
        phase += 2

    for h in range(parts):
        arrived(gath.at[h, 0], h, phase - 1)
        out[0, h] = gath[h, 0].astype(F32)
    drain(0)


def per_device(rhs, dinv, tiles, pattern):
    levels, _, nrhs, bs = rhs.shape
    rows, cols = lax.axis_size("row"), lax.axis_size("col")
    rep, parts, groups = rows // cols, PARTS, GROUPS
    gr, slots = nrhs // (parts * groups), tiles.shape[2]
    pairs = levels - 1
    phases = 2 * pairs + 2 * pairs
    out = pl.pallas_call(
        functools.partial(kernel, (levels, rows, cols, rep, parts, groups, gr, bs)),
        out_shape=jax.ShapeDtypeStruct((levels, parts, groups, gr, bs), F32),
        in_specs=[pl.BlockSpec(memory_space=pl.ANY)] * 4,
        out_specs=pl.BlockSpec(memory_space=pltpu.VMEM),
        scratch_shapes=[
            pltpu.SMEM((2, pairs, slots), jnp.int32),
            pltpu.VMEM((levels, parts, groups, gr, bs), BF16),
            pltpu.VMEM((levels, bs, bs), BF16),
            pltpu.VMEM((pairs, slots, bs, bs), BF16),
            pltpu.SemaphoreType.DMA((5,)),
            pltpu.VMEM((parts, pairs, gr, bs), F32),
            pltpu.VMEM((parts, groups * gr, bs), BF16),
            pltpu.VMEM((parts, 2 * pairs, gr, bs), BF16),
            [[pltpu.VMEM((rep, groups * gr, bs), BF16) for _ in range(parts)]]
            + [[pltpu.VMEM((rep, groups, gr, bs), BF16) for _ in range(parts)] for _ in range(pairs - 1)],
            pltpu.VMEM((parts, pairs, groups, gr, bs), BF16),
            pltpu.VMEM((parts, pairs, cols, gr, bs), BF16),
            pltpu.VMEM((parts, cols, groups, gr, bs), BF16),
            pltpu.VMEM((parts, pairs, rep, groups, gr, bs), BF16),
            pltpu.VMEM((parts, pairs, rows, gr, bs), BF16),
            pltpu.VMEM((parts, pairs, groups, gr, bs), BF16),
            pltpu.SemaphoreType.DMA((parts, phases)),
            pltpu.SemaphoreType.DMA((parts, phases)),
        ],
        compiler_params=pltpu.CompilerParams(
            collective_id=0, has_side_effects=True, vmem_limit_bytes=16 * 2**20
        ),
    )(
        *[
            pltpu.with_memory_space_constraint(a, pltpu.HBM)
            for a in (
                pattern[:, :, 0, :],
                rhs.reshape(levels, parts, groups, gr, bs),
                dinv.reshape(levels, bs, bs),
                tiles.reshape(pairs, slots, bs, bs),
            )
        ]
    )
    return out.reshape(levels, 1, nrhs, bs)


def solution(mesh):
    in_specs = (
        P(None, "row", None, None),
        P(None, "row", None, None),
        P(None, "row", "col", None, None),
        P(None, None, "row", "col"),
    )
    return jax.shard_map(
        per_device, mesh=mesh, in_specs=in_specs, out_specs=P(None, "row", None, None), check_vma=False
    )
```

```python
import functools

import jax
import jax.numpy as jnp
from jax import lax
from jax.experimental import pallas as pl
from jax.experimental.pallas import tpu as pltpu
from jax.sharding import PartitionSpec as P

MESH = pl.DeviceIdType.MESH
BF16, F32 = jnp.bfloat16, jnp.float32
NT = (((1,), (1,)), ((), ()))
NN = (((1,), (0,)), ((), ()))
NY = 4
GROUPS = 1
PARTS = 4


def mm(a, b, dims):
    return lax.dot_general(a, b, dims, preferred_element_type=F32)


def ring(k, n):
    return min(k % n, n - k % n)


def add_up(ref, n):
    total = ref[0].astype(F32)
    for k in range(1, n):
        total = total + ref[k].astype(F32)
    return total


def kernel(
    dims,
    pat_hbm, rhs_hbm, dinv_hbm, tiles_hbm, out,
    pat, rhs, dinv, tiles, load_sem,
    fwd, first, own, spread, part, red_f, red_a, part_b, red_b, gath,
    send_sem, recv_sem,
):
    levels, rows, cols, rep, parts, groups, gr, bs = dims
    nrhs = groups * gr
    slots = tiles.shape[1]
    nx, ny = cols // NY, NY
    me_r, me_c = lax.axis_index("row"), lax.axis_index("col")
    x, y = me_c // ny, lax.rem(me_c, ny)
    home = lax.rem(me_r, cols)
    blk_own = me_r // cols
    at_home = home == me_c
    home_x, home_y = home // ny, lax.rem(home, ny)
    g_own = lax.rem(x + nx - home_x, nx)
    is_owner = jnp.logical_and(home_y == y, g_own < groups)
    g_own = jnp.minimum(g_own, groups - 1)
    barrier = pltpu.get_barrier_semaphore()

    def each(body):
        def step(h, carry):
            body(h)
            return carry

        lax.fori_loop(0, parts, step, 0)


    def tell(r, c):
        pl.semaphore_signal(barrier, inc=1, device_id=(r, c), device_id_type=MESH)

    along = sorted(range(rows), key=lambda k: -ring(k // 2, rows // 2))
    plane = sorted(
        ((dx, dy) for dx in range(nx) for dy in range(ny)), key=lambda d: -2 * ring(d[1], ny) - ring(d[0], nx)
    )

    def at_row(k):
        return lax.rem(me_r + k, rows)

    def at_plane(d):
        return lax.rem(x + d[0], nx) * ny + lax.rem(y + d[1], ny)

    for blk in range(rep):
        tell(me_c + cols * blk, me_c)

    loads = [
        pltpu.make_async_copy(rhs_hbm, rhs, load_sem.at[0]),
        pltpu.make_async_copy(dinv_hbm.at[0], dinv.at[0], load_sem.at[1]),
        pltpu.make_async_copy(pat_hbm, pat, load_sem.at[2]),
        pltpu.make_async_copy(tiles_hbm, tiles, load_sem.at[3]),
        pltpu.make_async_copy(dinv_hbm.at[pl.ds(1, levels - 1)], dinv.at[pl.ds(1, levels - 1)], load_sem.at[4]),
    ]
    for load in loads:
        load.start()

    @pl.when(is_owner)
    def _():
        for d in plane:
            tell(me_r, at_plane(d))

    waits = []

    def drain(lag):
        while len(waits) > lag:
            for wait in waits.pop(0):
                wait()

    def send(src, dst, h, phase, r, c):
        pltpu.make_async_remote_copy(
            src_ref=src, dst_ref=dst, send_sem=send_sem.at[h, phase], recv_sem=recv_sem.at[h, phase],
            device_id=(r, c), device_id_type=MESH,
        ).start()

    def keep(src, dst, h, phase):
        pltpu.make_async_copy(src, dst, recv_sem.at[h, phase]).start()

    def arrived(ref, h, phase):
        pltpu.make_async_copy(ref, ref, recv_sem.at[h, phase]).wait()

    def sent(phase, *pieces):
        def wait(h, units, when):
            def act():
                left = units
                while left:
                    n = min(left, rows)
                    ref = red_b.at[0, 0, pl.ds(0, n)]
                    pltpu.make_async_copy(ref, ref, send_sem.at[h, phase]).wait()
                    left -= n

            return act if when is None else lambda: pl.when(when)(act)

        waits.append([wait(h, *piece) for h in range(parts) for piece in pieces])

    loads[0].wait()
    loads[1].wait()
    phase = 0

    @pl.when(at_home)
    def _():
        solved = mm(rhs[0].reshape(parts * nrhs, bs), dinv[0], NT)
        first[...] = solved.astype(BF16).reshape(parts, nrhs, bs)
        pl.semaphore_wait(barrier, rows + groups)
        @each
        def _(h, phase=phase):
            src, dst = first.at[h], spread[0].at[h, blk_own]
            for k in along:
                if k:
                    send(src, dst, h, 0, at_row(k), me_c)
            keep(src, dst, h, 0)

    @pl.when(jnp.logical_not(at_home))
    def _():
        pl.semaphore_wait(barrier, groups)

    @pl.when(is_owner)
    def _():
        @each
        def _(h, phase=phase):
            fwd[h, 0] = mm(rhs[0, h, g_own], dinv[0], NT)

    loads[2].wait()
    loads[3].wait()
    loads[4].wait()
    sent(0, ((rows - 1) * groups, at_home))
    phase = 1

    for level in range(1, levels):
        sp = level - 1
        if level > 1:
            @pl.when(is_owner)
            def _(phase=phase, sp=sp):
                @each
                def _(h, phase=phase):
                    arrived(red_f.at[h, sp - 1], h, phase - 1)
                    current = rhs[sp, h, g_own].astype(F32) - add_up(red_f.at[h, sp - 1], cols)
                    solved = mm(current.astype(BF16), dinv[sp], NT)
                    fwd[h, sp] = solved
                    own[h, sp] = solved.astype(BF16)
                    src, dst = own.at[h, sp], spread[sp].at[h, blk_own, g_own]
                    for k in along:
                        if k:
                            send(src, dst, h, phase, at_row(k), home)

                    @pl.when(at_home)
                    def _(src=src, dst=dst, h=h):
                        keep(src, dst, h, phase)

                    @pl.when(jnp.logical_not(at_home))
                    def _(src=src, dst=dst, h=h):
                        send(src, dst, h, phase, me_r, home)

            sent(phase, (rows - 1, is_owner), (1, jnp.logical_and(is_owner, jnp.logical_not(at_home))))
            drain(2)
            phase += 1
        @each
        def _(h, phase=phase):
            arrived(spread[sp].at[h], h, phase - 1)
            total = None
            for slot in range(slots):
                blk = pat[1, sp, slot] // cols
                source = spread[sp][h, 0]
                for other in range(1, rep):
                    source = jnp.where(blk == other, spread[sp][h, other], source)
                source = source.reshape(nrhs, bs)
                product = mm(source, tiles[sp, slot], NT)
                total = product if total is None else total + product
            part[h, sp] = total.astype(BF16).reshape(groups, gr, bs)
            if level < levels - 1:
                for g in range(groups):
                    src, dst = part.at[h, sp, g], red_f.at[h, sp, me_c]
                    col = lax.rem(home_x + g, nx) * ny + home_y

                    @pl.when(col == me_c)
                    def _(src=src, dst=dst, phase=phase, h=h):
                        keep(src, dst, h, phase)

                    @pl.when(col != me_c)
                    def _(src=src, dst=dst, phase=phase, h=h, col=col):
                        send(src, dst, h, phase, me_r, col)

            else:
                for d in plane:
                    if d != (0, 0):
                        send(part.at[h, sp], red_a.at[h, me_c], h, phase, me_r, at_plane(d))
                keep(part.at[h, sp], red_a.at[h, me_c], h, phase)

        if level < levels - 1:
            sent(phase, (groups - 1, None), (1, jnp.logical_not(is_owner)))
        else:
            sent(phase, ((cols - 1) * groups, None))
        drain(2)
        phase += 1

    for level in range(levels - 2, -1, -1):
        @each
        def _(h, phase=phase):
            if level == levels - 2:
                arrived(red_a.at[h], h, phase - 1)
                current = rhs[level + 1, h].astype(F32) - add_up(red_a.at[h], cols)
                remainder = mm(current.astype(BF16).reshape(nrhs, bs), dinv[level + 1], NT)
                solved = mm(remainder.astype(BF16), dinv[level + 1], NN)
                out[level + 1, h] = solved.reshape(groups, gr, bs)
                source = solved.astype(BF16)
            else:
                arrived(gath.at[h, level + 1], h, phase - 1)
                source = gath[h, level + 1].reshape(nrhs, bs)
            products = [mm(source, tiles[level, slot], NN) for slot in range(slots)]
            for blk in range(rep):
                total = None
                for slot in range(slots):
                    hit = pat[1, level, slot] // cols == blk
                    term = jnp.where(hit, products[slot], 0.0)
                    total = term if total is None else total + term
                part_b[h, level, blk] = total.astype(BF16).reshape(groups, gr, bs)
            for g in range(groups - 1, -1, -1):
                for blk in range(rep):
                    row = me_c + cols * blk
                    src, dst = part_b.at[h, level, blk, g], red_b.at[h, level, me_r]
                    if g:
                        send(src, dst, h, phase, row, lax.rem(x + g, nx) * ny + y)
                    else:
                        @pl.when(row == me_r)
                        def _(src=src, dst=dst, phase=phase, h=h):
                            keep(src, dst, h, phase)

                        @pl.when(row != me_r)
                        def _(src=src, dst=dst, phase=phase, row=row, h=h):
                            send(src, dst, h, phase, row, me_c)

            if level < levels - 2:
                out[level + 1, h] = gath[h, level + 1].astype(F32)

        sent(phase, (rep * groups - 1, None), (1, jnp.logical_not(at_home)))
        drain(2)

        @pl.when(is_owner)
        def _(level=level, phase=phase):
            @each
            def _(h, phase=phase):
                arrived(red_b.at[h, level], h, phase)
                remainder = fwd[h, level] - add_up(red_b.at[h, level], rows)
                solved = mm(remainder.astype(BF16), dinv[level], NN)
                own[h, levels - 1 + level] = solved.astype(BF16)
                src, dst = own.at[h, levels - 1 + level], gath.at[h, level, g_own]
                for d in plane:
                    if d != (0, 0):
                        send(src, dst, h, phase + 1, me_r, at_plane(d))
                keep(src, dst, h, phase + 1)

        sent(phase + 1, (cols - 1, is_owner))
        drain(1 if level == 0 else 2)
        phase += 2

    @each
    def _(h, phase=phase):
        arrived(gath.at[h, 0], h, phase - 1)
        out[0, h] = gath[h, 0].astype(F32)
    drain(0)


def per_device(rhs, dinv, tiles, pattern):
    levels, _, nrhs, bs = rhs.shape
    rows, cols = lax.axis_size("row"), lax.axis_size("col")
    rep, parts, groups = rows // cols, PARTS, GROUPS
    gr, slots = nrhs // (parts * groups), tiles.shape[2]
    pairs = levels - 1
    phases = 2 * pairs + 2 * pairs
    out = pl.pallas_call(
        functools.partial(kernel, (levels, rows, cols, rep, parts, groups, gr, bs)),
        out_shape=jax.ShapeDtypeStruct((levels, parts, groups, gr, bs), F32),
        in_specs=[pl.BlockSpec(memory_space=pl.ANY)] * 4,
        out_specs=pl.BlockSpec(memory_space=pltpu.VMEM),
        scratch_shapes=[
            pltpu.SMEM((2, pairs, slots), jnp.int32),
            pltpu.VMEM((levels, parts, groups, gr, bs), BF16),
            pltpu.VMEM((levels, bs, bs), BF16),
            pltpu.VMEM((pairs, slots, bs, bs), BF16),
            pltpu.SemaphoreType.DMA((5,)),
            pltpu.VMEM((parts, pairs, gr, bs), F32),
            pltpu.VMEM((parts, groups * gr, bs), BF16),
            pltpu.VMEM((parts, 2 * pairs, gr, bs), BF16),
            [pltpu.VMEM((parts, rep, groups * gr, bs), BF16)]
            + [pltpu.VMEM((parts, rep, groups, gr, bs), BF16) for _ in range(pairs - 1)],
            pltpu.VMEM((parts, pairs, groups, gr, bs), BF16),
            pltpu.VMEM((parts, pairs, cols, gr, bs), BF16),
            pltpu.VMEM((parts, cols, groups, gr, bs), BF16),
            pltpu.VMEM((parts, pairs, rep, groups, gr, bs), BF16),
            pltpu.VMEM((parts, pairs, rows, gr, bs), BF16),
            pltpu.VMEM((parts, pairs, groups, gr, bs), BF16),
            pltpu.SemaphoreType.DMA((parts, phases)),
            pltpu.SemaphoreType.DMA((parts, phases)),
        ],
        compiler_params=pltpu.CompilerParams(
            collective_id=0, has_side_effects=True, vmem_limit_bytes=16 * 2**20
        ),
    )(
        *[
            pltpu.with_memory_space_constraint(a, pltpu.HBM)
            for a in (
                pattern[:, :, 0, :],
                rhs.reshape(levels, parts, groups, gr, bs),
                dinv.reshape(levels, bs, bs),
                tiles.reshape(pairs, slots, bs, bs),
            )
        ]
    )
    return out.reshape(levels, 1, nrhs, bs)


def solution(mesh):
    in_specs = (
        P(None, "row", None, None),
        P(None, "row", None, None),
        P(None, "row", "col", None, None),
        P(None, None, "row", "col"),
    )
    return jax.shard_map(
        per_device, mesh=mesh, in_specs=in_specs, out_specs=P(None, "row", None, None), check_vma=False
    )
```

```python
import functools

import jax
import jax.numpy as jnp
from jax import lax
from jax.experimental import pallas as pl
from jax.experimental.pallas import tpu as pltpu
from jax.sharding import PartitionSpec as P

MESH = pl.DeviceIdType.MESH
BF16, F32 = jnp.bfloat16, jnp.float32
NT = (((1,), (1,)), ((), ()))
NN = (((1,), (0,)), ((), ()))
NY = 4
GROUPS = 1
PARTS = 4


def mm(a, b, dims):
    return lax.dot_general(a, b, dims, preferred_element_type=F32)


def ring(k, n):
    return min(k % n, n - k % n)


def add_up(ref, n):
    total = ref[0].astype(F32)
    for k in range(1, n):
        total = total + ref[k].astype(F32)
    return total


def kernel(
    dims,
    pat_hbm, rhs_hbm, dinv_hbm, tiles_hbm, out,
    pat, rhs, dinv, tiles, load_sem,
    fwd, first, own, spread, part, red_f, red_a, part_b, red_b, gath,
    send_sem, recv_sem,
):
    levels, rows, cols, rep, parts, groups, gr, bs = dims
    nrhs = groups * gr
    slots = tiles.shape[1]
    nx, ny = cols // NY, NY
    me_r, me_c = lax.axis_index("row"), lax.axis_index("col")
    x, y = me_c // ny, lax.rem(me_c, ny)
    home = lax.rem(me_r, cols)
    blk_own = me_r // cols
    at_home = home == me_c
    home_x, home_y = home // ny, lax.rem(home, ny)
    g_own = lax.rem(x + nx - home_x, nx)
    is_owner = jnp.logical_and(home_y == y, g_own < groups)
    g_own = jnp.minimum(g_own, groups - 1)
    barrier = pltpu.get_barrier_semaphore()

    def each(body):
        def step(h, carry):
            body(h)
            return carry

        lax.fori_loop(0, parts, step, 0)


    def tell(r, c):
        pl.semaphore_signal(barrier, inc=1, device_id=(r, c), device_id_type=MESH)

    along = sorted(range(rows), key=lambda k: -ring(k // 2, rows // 2))
    plane = sorted(
        ((dx, dy) for dx in range(nx) for dy in range(ny)), key=lambda d: -2 * ring(d[1], ny) - ring(d[0], nx)
    )

    far_blk = lax.rem((me_r + rows + rows // 2 + cols // 2 - me_c) // cols, rep)

    def at_row(k):
        return lax.rem(me_r + k, rows)

    def at_plane(d):
        return lax.rem(x + d[0], nx) * ny + lax.rem(y + d[1], ny)

    for blk in range(rep):
        tell(me_c + cols * blk, me_c)

    loads = [
        pltpu.make_async_copy(rhs_hbm, rhs, load_sem.at[0]),
        pltpu.make_async_copy(dinv_hbm.at[0], dinv.at[0], load_sem.at[1]),
        pltpu.make_async_copy(pat_hbm, pat, load_sem.at[2]),
        pltpu.make_async_copy(tiles_hbm, tiles, load_sem.at[3]),
        pltpu.make_async_copy(dinv_hbm.at[pl.ds(1, levels - 1)], dinv.at[pl.ds(1, levels - 1)], load_sem.at[4]),
    ]
    for load in loads:
        load.start()

    @pl.when(is_owner)
    def _():
        for d in plane:
            tell(me_r, at_plane(d))

    waits = []

    def drain(lag):
        while len(waits) > lag:
            for wait in waits.pop(0):
                wait()

    def send(src, dst, h, phase, r, c):
        pltpu.make_async_remote_copy(
            src_ref=src, dst_ref=dst, send_sem=send_sem.at[h, phase], recv_sem=recv_sem.at[h, phase],
            device_id=(r, c), device_id_type=MESH,
        ).start()

    def keep(src, dst, h, phase):
        pltpu.make_async_copy(src, dst, recv_sem.at[h, phase]).start()

    def arrived(ref, h, phase):
        pltpu.make_async_copy(ref, ref, recv_sem.at[h, phase]).wait()

    def sent(phase, *pieces):
        def wait(h, units, when):
            def act():
                left = units
                while left:
                    n = min(left, rows)
                    ref = red_b.at[0, 0, pl.ds(0, n)]
                    pltpu.make_async_copy(ref, ref, send_sem.at[h, phase]).wait()
                    left -= n

            return act if when is None else lambda: pl.when(when)(act)

        waits.append([wait(h, *piece) for h in range(parts) for piece in pieces])

    loads[0].wait()
    loads[1].wait()
    phase = 0

    @pl.when(at_home)
    def _():
        solved = mm(rhs[0].reshape(parts * nrhs, bs), dinv[0], NT)
        first[...] = solved.astype(BF16).reshape(parts, nrhs, bs)
        pl.semaphore_wait(barrier, rows + groups)
        @each
        def _(h, phase=phase):
            src, dst = first.at[h], spread[0].at[h, blk_own]
            for k in along:
                if k:
                    send(src, dst, h, 0, at_row(k), me_c)
            keep(src, dst, h, 0)

    @pl.when(jnp.logical_not(at_home))
    def _():
        pl.semaphore_wait(barrier, groups)

    @pl.when(is_owner)
    def _():
        @each
        def _(h, phase=phase):
            fwd[h, 0] = mm(rhs[0, h, g_own], dinv[0], NT)

    loads[2].wait()
    loads[3].wait()
    loads[4].wait()
    sent(0, ((rows - 1) * groups, at_home))
    phase = 1

    for level in range(1, levels):
        sp = level - 1
        if level > 1:
            @pl.when(is_owner)
            def _(phase=phase, sp=sp):
                @each
                def _(h, phase=phase):
                    arrived(red_f.at[h, sp - 1], h, phase - 1)
                    current = rhs[sp, h, g_own].astype(F32) - add_up(red_f.at[h, sp - 1], cols)
                    solved = mm(current.astype(BF16), dinv[sp], NT)
                    fwd[h, sp] = solved
                    own[h, sp] = solved.astype(BF16)
                    src, dst = own.at[h, sp], spread[sp].at[h, blk_own, g_own]
                    for k in along:
                        if k:
                            send(src, dst, h, phase, at_row(k), home)

                    @pl.when(at_home)
                    def _(src=src, dst=dst, h=h):
                        keep(src, dst, h, phase)

                    @pl.when(jnp.logical_not(at_home))
                    def _(src=src, dst=dst, h=h):
                        send(src, dst, h, phase, me_r, home)

            sent(phase, (rows - 1, is_owner), (1, jnp.logical_and(is_owner, jnp.logical_not(at_home))))
            drain(2)
            phase += 1
        @each
        def _(h, phase=phase):
            arrived(spread[sp].at[h], h, phase - 1)
            total = None
            for slot in range(slots):
                blk = pat[1, sp, slot] // cols
                source = spread[sp][h, 0]
                for other in range(1, rep):
                    source = jnp.where(blk == other, spread[sp][h, other], source)
                source = source.reshape(nrhs, bs)
                product = mm(source, tiles[sp, slot], NT)
                total = product if total is None else total + product
            part[h, sp] = total.astype(BF16).reshape(groups, gr, bs)
            if level < levels - 1:
                for g in range(groups):
                    src, dst = part.at[h, sp, g], red_f.at[h, sp, me_c]
                    col = lax.rem(home_x + g, nx) * ny + home_y

                    @pl.when(col == me_c)
                    def _(src=src, dst=dst, phase=phase, h=h):
                        keep(src, dst, h, phase)

                    @pl.when(col != me_c)
                    def _(src=src, dst=dst, phase=phase, h=h, col=col):
                        send(src, dst, h, phase, me_r, col)

            else:
                for d in plane:
                    if d != (0, 0):
                        send(part.at[h, sp], red_a.at[h, me_c], h, phase, me_r, at_plane(d))
                keep(part.at[h, sp], red_a.at[h, me_c], h, phase)

        if level < levels - 1:
            sent(phase, (groups - 1, None), (1, jnp.logical_not(is_owner)))
        else:
            sent(phase, ((cols - 1) * groups, None))
        drain(2)
        phase += 1

    for level in range(levels - 2, -1, -1):
        @each
        def _(h, phase=phase):
            if level == levels - 2:
                arrived(red_a.at[h], h, phase - 1)
                current = rhs[level + 1, h].astype(F32) - add_up(red_a.at[h], cols)
                remainder = mm(current.astype(BF16).reshape(nrhs, bs), dinv[level + 1], NT)
                solved = mm(remainder.astype(BF16), dinv[level + 1], NN)
                out[level + 1, h] = solved.reshape(groups, gr, bs)
                source = solved.astype(BF16)
            else:
                arrived(gath.at[h, level + 1], h, phase - 1)
                source = gath[h, level + 1].reshape(nrhs, bs)
            products = [mm(source, tiles[level, slot], NN) for slot in range(slots)]
            for blk in range(rep):
                total = None
                for slot in range(slots):
                    hit = pat[1, level, slot] // cols == blk
                    term = jnp.where(hit, products[slot], 0.0)
                    total = term if total is None else total + term
                part_b[h, level, blk] = total.astype(BF16).reshape(groups, gr, bs)
            for g in range(groups - 1, -1, -1):
                for k in range(rep):
                    blk = lax.rem(far_blk + k, rep)
                    row = me_c + cols * blk
                    src, dst = part_b.at[h, level, blk, g], red_b.at[h, level, me_r]
                    if g:
                        send(src, dst, h, phase, row, lax.rem(x + g, nx) * ny + y)
                    else:
                        @pl.when(row == me_r)
                        def _(src=src, dst=dst, phase=phase, h=h):
                            keep(src, dst, h, phase)

                        @pl.when(row != me_r)
                        def _(src=src, dst=dst, phase=phase, row=row, h=h):
                            send(src, dst, h, phase, row, me_c)

            if level < levels - 2:
                out[level + 1, h] = gath[h, level + 1].astype(F32)

        sent(phase, (rep * groups - 1, None), (1, jnp.logical_not(at_home)))
        drain(2)

        @pl.when(is_owner)
        def _(level=level, phase=phase):
            @each
            def _(h, phase=phase):
                arrived(red_b.at[h, level], h, phase)
                remainder = fwd[h, level] - add_up(red_b.at[h, level], rows)
                solved = mm(remainder.astype(BF16), dinv[level], NN)
                own[h, levels - 1 + level] = solved.astype(BF16)
                src, dst = own.at[h, levels - 1 + level], gath.at[h, level, g_own]
                for d in plane:
                    if d != (0, 0):
                        send(src, dst, h, phase + 1, me_r, at_plane(d))
                keep(src, dst, h, phase + 1)

        sent(phase + 1, (cols - 1, is_owner))
        drain(1 if level == 0 else 2)
        phase += 2

    @each
    def _(h, phase=phase):
        arrived(gath.at[h, 0], h, phase - 1)
        out[0, h] = gath[h, 0].astype(F32)
    drain(0)


def per_device(rhs, dinv, tiles, pattern):
    levels, _, nrhs, bs = rhs.shape
    rows, cols = lax.axis_size("row"), lax.axis_size("col")
    rep, parts, groups = rows // cols, PARTS, GROUPS
    gr, slots = nrhs // (parts * groups), tiles.shape[2]
    pairs = levels - 1
    phases = 2 * pairs + 2 * pairs
    out = pl.pallas_call(
        functools.partial(kernel, (levels, rows, cols, rep, parts, groups, gr, bs)),
        out_shape=jax.ShapeDtypeStruct((levels, parts, groups, gr, bs), F32),
        in_specs=[pl.BlockSpec(memory_space=pl.ANY)] * 4,
        out_specs=pl.BlockSpec(memory_space=pltpu.VMEM),
        scratch_shapes=[
            pltpu.SMEM((2, pairs, slots), jnp.int32),
            pltpu.VMEM((levels, parts, groups, gr, bs), BF16),
            pltpu.VMEM((levels, bs, bs), BF16),
            pltpu.VMEM((pairs, slots, bs, bs), BF16),
            pltpu.SemaphoreType.DMA((5,)),
            pltpu.VMEM((parts, pairs, gr, bs), F32),
            pltpu.VMEM((parts, groups * gr, bs), BF16),
            pltpu.VMEM((parts, 2 * pairs, gr, bs), BF16),
            [pltpu.VMEM((parts, rep, groups * gr, bs), BF16)]
            + [pltpu.VMEM((parts, rep, groups, gr, bs), BF16) for _ in range(pairs - 1)],
            pltpu.VMEM((parts, pairs, groups, gr, bs), BF16),
            pltpu.VMEM((parts, pairs, cols, gr, bs), BF16),
            pltpu.VMEM((parts, cols, groups, gr, bs), BF16),
            pltpu.VMEM((parts, pairs, rep, groups, gr, bs), BF16),
            pltpu.VMEM((parts, pairs, rows, gr, bs), BF16),
            pltpu.VMEM((parts, pairs, groups, gr, bs), BF16),
            pltpu.SemaphoreType.DMA((parts, phases)),
            pltpu.SemaphoreType.DMA((parts, phases)),
        ],
        compiler_params=pltpu.CompilerParams(
            collective_id=0, has_side_effects=True, vmem_limit_bytes=16 * 2**20
        ),
    )(
        *[
            pltpu.with_memory_space_constraint(a, pltpu.HBM)
            for a in (
                pattern[:, :, 0, :],
                rhs.reshape(levels, parts, groups, gr, bs),
                dinv.reshape(levels, bs, bs),
                tiles.reshape(pairs, slots, bs, bs),
            )
        ]
    )
    return out.reshape(levels, 1, nrhs, bs)


def solution(mesh):
    in_specs = (
        P(None, "row", None, None),
        P(None, "row", None, None),
        P(None, "row", "col", None, None),
        P(None, None, "row", "col"),
    )
    return jax.shard_map(
        per_device, mesh=mesh, in_specs=in_specs, out_specs=P(None, "row", None, None), check_vma=False
    )
```
